128 devices in a mesh: lat: 16 (over x, y), lon: 8 (over z, core).
Axes of the slice: x: 4, y: 4, z: 4, core: 2. Of those that a mesh axis runs over, the one named last changes fastest.
Arguments:
- cotangent: bfloat16 [16384, 16, 128], P(('lat', 'lon')), may hold values from -6 to 6
- fractions: float32 [16384, 2, 128], P(('lat', 'lon')), may hold values from 0 to 1
- offsets: int32 [16384, 2, 128], P(('lat', 'lon')), may hold values from 0 to 7
- owner: int32 [16384, 1], P(('lat', 'lon')), may hold values from 0 to 127; in each aligned block of 128 rows (0 to 127, 128 to 255, ...) at most 2 rows name the same one
- sub_block: int32 [16384], P(('lat', 'lon')), may hold values from 0 to 255
- lon_inverse: float32 [2048, 2048], replicated, may hold values from -0.125 to 0.125
- lat_inverse: float32 [1024, 1024], replicated, may hold values from -0.1875 to 0.1875
Outputs:
- tracer_adjoint: float32 [16, 1024, 2048], P('lon', None, 'lat')
The draws below stay inside these ranges and needn't reach their ends.
Inputs may be any that keep to these rules, and one draw needn't show every extreme that they name: Among the 128 arrival blocks of one device no owner is named more than 2 times; some owner is named exactly 2 times.
All inputs are finite; a program needn't handle non-finite values.
Results may differ from the reference program's by a relative error of at most 0.0029.
The reference program's roundings to bfloat16 on the way (of `stencil` and `window`) count: a program that leaves them out, or rounds other values in their place, can miss the bound.
Values may be sent and summed in bfloat16 or wider, within the bound.
A program may use at most 128 MiB of HBM per device.

```python
import math
import jax
import jax.numpy as jnp
import numpy as np
from jax import lax

C = 16
BS = 8
CLAT = 64
CLON = 256
NB = 128
R = 128
CAP = 2
SB = 256
NLAT = 1024
NLON = 2048
BLOCKS = 16384
N_LAT = 16
N_LON = 8
DEVICES = 128


def plant(result, stream_key, smallest, largest):
    place = [jax.random.randint(jax.random.fold_in(stream_key, axis), (), 0, length) for axis, length in enumerate(result.shape)]
    longest = result.shape.index(max(result.shape))
    beside = place[:longest] + [(place[longest] + 1) % result.shape[longest]] + place[longest + 1:]
    return result.at[tuple(place)].set(smallest).at[tuple(beside)].set(largest)


def steps_of(own_key, shape, split, smallest, top_value):
    def one(position, blocks):
        heights = jax.random.uniform(jax.random.fold_in(jax.random.fold_in(own_key, 6), position), (blocks,), jnp.float32, smallest / len(split), top_value / len(split))
        return jnp.repeat(jnp.exp(heights), shape[position] // blocks).reshape((-1,) + (1,) * (len(shape) - position - 1))

    loudness = one(*split[0])
    for cut in split[1:]:
        loudness = loudness * one(*cut)
    return loudness


def routed_block(stream_key, own, number, rows, number_of, top, limit, slope):
    order = jax.random.permutation(stream_key, number_of)
    packed, ordinary = load_shares(number_of, rows * top, limit, slope, True), load_shares(number_of, rows * top, limit, slope, False)
    places = jnp.arange(number_of)

    def named(tallies, rotation):
        used = int((tallies > 0).sum())
        fixed = max(1, used // 4)
        shifted = fixed + (places - fixed + rotation * (used - fixed)) % max(1, number_of - fixed)
        return jnp.zeros((number_of,), jnp.int32).at[order[jnp.where(places < fixed, places, shifted)]].set(jnp.asarray(tallies, jnp.int32))

    tallies = jnp.where(number % 4 == 0, named(packed, number // 4), named(ordinary, number - number // 4 - 1))
    mixed = jax.random.permutation(jax.random.fold_in(own, 3), number_of)
    giver, receiver = mixed[0:number_of // 2 * 2:2], mixed[1:number_of // 2 * 2:2]
    slack = jnp.minimum(tallies[giver] - 1, limit - tallies[receiver]) // 2
    slack = jnp.where((giver == order[0]) | (receiver == order[0]) | (tallies[receiver] == 0), 0, jnp.maximum(slack, 0))
    shifted = jax.random.randint(jax.random.fold_in(own, 4), (number_of // 2,), 0, 1 << 20) % (slack + 1)
    tallies = tallies.at[giver].add(-shifted).at[receiver].add(shifted)
    labels = jnp.searchsorted(jnp.cumsum(tallies), jnp.arange(rows * top), side="right").astype(jnp.int32)
    table = labels.reshape(top, rows).T
    table = table[jax.random.permutation(jax.random.fold_in(own, 1), rows)]
    rotation = jax.random.randint(jax.random.fold_in(own, 2), (rows, 1), 0, top)
    return jnp.take_along_axis(table, (jnp.arange(top)[None, :] + rotation) % top, axis=1)


def load_shares(count, total, most, slope, full):
    portions = [(1 << 20) // math.isqrt(rank ** slope) + 1 for rank in range(1, count + 1)]
    largest = most if full else min(most, max(-(-total // count), total * portions[0] // sum(portions)))
    least = 1 if total - largest >= count - 1 else 0
    given, surplus = [largest] + [least] * (count - 1), total - largest - least * (count - 1)
    while surplus > 0:
        free = [i for i in range(1, count) if given[i] < largest] or [i for i in range(1, count) if given[i] < most]
        pool, remaining = sum([portions[i] for i in free]), surplus
        for i in free:
            more = min(most - given[i], max(1, remaining * portions[i] // pool), surplus)
            given[i] = given[i] + more
            surplus = surplus - more
    return np.array(given)


def bell_draw(rng, shape, width, limit, shards=(), held_as=jnp.bfloat16):
    entries = jax.random.normal(rng, shape, jnp.float32) * width
    if len(shards) > 0:
        entries = steps_of(rng, shape, shards, -0.22, 0.18) * entries
    return jnp.clip(entries, min=-limit, max=limit).astype(held_as)


def setup_inputs(seed: int = 0) -> dict:
    key_of = jax.random.split(jax.random.key(seed), 8)
    cotangent = bell_draw(key_of[0], (BLOCKS, C, R), 1.0, 6.0, ((0, 128),))
    fractions = jnp.clip(1.0 * jax.random.uniform(key_of[1], (BLOCKS, 2, R), jnp.float32) ** steps_of(key_of[1], (BLOCKS, 2, R), ((0, 128),), -0.2, 0.2), 0.0, 1.0)
    offsets = plant(jax.random.randint(key_of[2], (BLOCKS, 2, R), 0, BS), jax.random.fold_in(key_of[2], 1), 0, BS - 1).astype(jnp.int32)
    owner_keys = jax.random.split(jax.random.fold_in(key_of[3], 1), BLOCKS // NB)
    owner_turns = jax.random.permutation(jax.random.fold_in(key_of[3], 3), BLOCKS // NB)
    owner = jax.vmap(lambda own, number: routed_block(jax.random.fold_in(key_of[3], 2), own, number, NB, DEVICES, 1, CAP, 2))(owner_keys, owner_turns).reshape((BLOCKS, 1))
    sub_block = plant(jax.random.randint(key_of[4], (BLOCKS,), 0, SB), jax.random.fold_in(key_of[4], 1), 0, SB - 1).astype(jnp.int32)
    lon_inverse = bell_draw(key_of[5], (NLON, NLON), NLON ** -0.5, 0.125, (), jnp.float32)
    lat_inverse = bell_draw(key_of[6], (NLAT, NLAT), NLAT ** -0.5, 0.1875, (), jnp.float32)
    return {"cotangent": cotangent, "fractions": fractions, "offsets": offsets, "owner": owner, "sub_block": sub_block, "lon_inverse": lon_inverse, "lat_inverse": lat_inverse}


def spline_weights(t):
    cube = t * t * t
    square = t * t
    return jnp.stack([(1.0 - t) ** 3 / 6.0, (3.0 * cube - 6.0 * square + 4.0) / 6.0, (-3.0 * cube + 3.0 * square + 3.0 * t + 1.0) / 6.0, cube / 6.0])


def window_table(frac, offset):
    weights = spline_weights(frac)
    places = jnp.arange(2 * BS, dtype=jnp.int32)
    table = jnp.zeros((frac.shape[0], 2 * BS, frac.shape[1]), jnp.float32)
    for step in range(4):
        match = (offset[:, None, :] + step) == places[None, :, None]
        table = table + jnp.where(match, weights[step][:, None, :], 0.0)
    return table


def device_windows(inputs):
    grads, frac, offset = inputs
    lat_table = window_table(frac[:, 0], offset[:, 0])
    lon_table = window_table(frac[:, 1], offset[:, 1])
    stencil = (lat_table[:, :, None, :] * lon_table[:, None, :, :]).reshape(frac.shape[0], 4 * BS * BS, frac.shape[2]).astype(jnp.bfloat16)
    window = jnp.einsum("bcr,bpr->bcp", grads.astype(jnp.float32), stencil.astype(jnp.float32))
    return window.astype(jnp.bfloat16)


def reference(cotangent, fractions, offsets, owner, sub_block, lon_inverse, lat_inverse):
    devices = N_LAT * N_LON
    windows = lax.map(device_windows, (cotangent.reshape(devices, NB, C, R), fractions.reshape(devices, NB, 2, R), offsets.reshape(devices, NB, 2, R)))
    windows = windows.reshape(BLOCKS, C, 2 * BS, 2 * BS).astype(jnp.float32)
    span = jnp.arange(2 * BS, dtype=jnp.int32)
    target = owner[:, 0]
    across = CLON // BS
    row0 = (target // N_LON) * CLAT + (sub_block // across) * BS - 1
    col0 = (target % N_LON) * CLON + (sub_block % across) * BS - 1
    row_index = (row0[:, None] + span[None, :] + BS).astype(jnp.int32)
    col_index = ((col0[:, None] + span[None, :]) % NLON).astype(jnp.int32)
    grid = jnp.zeros((C, NLAT + 2 * BS, NLON), jnp.float32)
    grid = grid.at[:, row_index[:, :, None], col_index[:, None, :]].add(jnp.transpose(windows, (1, 0, 2, 3)))
    coeff_adjoint = grid[:, BS:BS + NLAT]
    lon_adjoint = jnp.dot(coeff_adjoint.reshape(C * NLAT, NLON), lon_inverse, precision=lax.Precision.HIGHEST).reshape(C, NLAT, NLON)
    return jnp.einsum("cjx,ji->cix", lon_adjoint, lat_inverse, precision=lax.Precision.HIGHEST)
```

```python
import jax
import jax.numpy as jnp
from jax import lax
from jax.experimental import pallas as pl
from jax.experimental.pallas import tpu as pltpu
from jax.sharding import PartitionSpec as P

MESH = pl.DeviceIdType.MESH
F32 = jnp.float32
BF16 = jnp.bfloat16
LATS = 16
LONS = 8
BLOCKS = 128
CHANS = 16
NLAT = 1024
NLON = 2048
PAIR = 16
LABEL = 127
BANDS = 9
ROWS = BANDS * 16


def partner(step, lat, lon):
    turn, hop = step // LATS, step % LATS
    x = (lat // 4 + hop // 4) % 4
    y = (lat % 4 + hop % 4) % 4
    z = (lon // 2 + turn // 2) % 4
    core = (lon % 2 + turn % 2) % 2
    return x * 4 + y, z * 2 + core


def spline(distance):
    size = jnp.abs(distance)
    far = jnp.maximum(2.0 - size, 0.0)
    near = jnp.maximum(1.0 - size, 0.0)
    return far * far * far - 4.0 * (near * near * near)


def wait_for(view, sem):
    pltpu.make_async_copy(view, view, sem).wait()


def sublane_places(first):
    row = lax.broadcasted_iota(jnp.int32, (8, 128), 0)
    return jnp.where(row < 3, row + 8, first(row)).astype(F32)


def kernel(cot_ref, frac_ref, off_ref, owner_ref, sub_ref, lon_ref, lat_ref, out_ref,
           lat_tab, windows, packed, got, summed, coeff, lon_raw, lon_half, lat_raw, lat_high,
           lat_low, lines, columns, column_sum,
           ready_sem, load_sem, send_sem, recv_sem, line_send, line_recv):
    lat, lon = lax.axis_index("lat"), lax.axis_index("lon")
    barrier = pltpu.get_barrier_semaphore()

    def greet(step, carry):
        lat_to, lon_to = partner(step, lat, lon)
        pl.semaphore_signal(barrier, inc=1, device_id=(lat_to, lon_to), device_id_type=MESH)
        return carry

    lax.fori_loop(1, LATS, greet, 0)
    lax.fori_loop(1, LONS, lambda turn, carry: greet(turn * LATS, carry), 0)

    for part in range(16):
        pltpu.make_async_copy(
            lon_ref.at[:, pl.ds(part * 128, 128)], lon_raw.at[part], load_sem.at[0]
        ).start()
    pltpu.make_async_copy(lat_ref, lat_raw, load_sem.at[1]).start()

    index = lax.broadcasted_iota(jnp.int32, (8, 128), 0)
    low = index.astype(F32)
    low_tail = index < 3
    ends_a = sublane_places(lambda row: row - 3)
    ends_b = sublane_places(lambda row: row + 2)
    ends_c = sublane_places(lambda row: jnp.where(row < 6, 10, 15))
    lat_c = jnp.where(low_tail, 6, jnp.where(index < 6, index + 5, 15)).astype(F32)

    def window_group(group, carry):
        places = off_ref[pl.ds(group * 8, 8)].astype(F32) + 1.0 + frac_ref[pl.ds(group * 8, 8)]
        for item in range(8):
            block = group * 8 + item
            centre_lat = jnp.broadcast_to(places[item, 0:1, :], (8, 128))
            centre_lon = jnp.broadcast_to(places[item, 1:2, :], (8, 128))
            lat_tab[item, 0:8, :] = spline(low - centre_lat) * (1.0 / 36.0)
            lat_tab[item, 8:16, :] = spline(low + 8.0 - centre_lat) * (1.0 / 36.0)
            lat_last = spline(lat_c - centre_lat) * (1.0 / 36.0)
            lon_head = spline(low - centre_lon)
            tail_a = spline(ends_a - centre_lon)
            tail_b = spline(ends_b - centre_lon)
            tail_c = spline(ends_c - centre_lon)

            def lat_row(w):
                return jnp.broadcast_to(lat_tab[item, w : w + 1, :], (8, 128))

            high_rows = [lat_row(8), lat_row(9), lat_row(10)]
            pieces = []
            for w in range(8):
                row = lat_row(w)
                if w < 6:
                    tail_lat = jnp.where(low_tail, row, high_rows[w % 3])
                elif w == 6:
                    tail_lat = lat_last
                else:
                    tail_lat = row
                tail_lon = tail_a if w < 3 else (tail_b if w < 6 else tail_c)
                pieces.append(row * lon_head)
                pieces.append(tail_lat * tail_lon)
            stencil = jnp.concatenate(pieces, axis=0).astype(BF16)
            window = lax.dot_general(
                cot_ref[block], stencil, (((1,), (1,)), ((), ())), preferred_element_type=F32
            )
            windows[pl.ds(pl.multiple_of(block * CHANS, CHANS), CHANS), :] = window
        return carry

    lax.fori_loop(0, 8, window_group, 0)

    pl.semaphore_wait(barrier, LATS - 1 + LONS - 1)

    def tell(step, carry):
        lat_to, lon_to = partner(step, lat, lon)
        pl.semaphore_signal(ready_sem, inc=1, device_id=(lat_to, lon_to), device_id_type=MESH)
        return carry

    lax.fori_loop(1, LATS, tell, 0)
    lax.fori_loop(8, 16, window_group, 0)

    own_down = jnp.broadcast_to(owner_ref[...].astype(F32), (BLOCKS, BLOCKS))
    own_across = own_down.T
    down = lax.broadcasted_iota(jnp.int32, (BLOCKS, BLOCKS), 0)
    across = lax.broadcasted_iota(jnp.int32, (BLOCKS, BLOCKS), 1)
    earlier = jnp.where((own_down == own_across) & (down < across), 1.0, 0.0)
    place = 2.0 * own_across[0:1, :] + jnp.sum(earlier, axis=0, keepdims=True)
    slot = lax.broadcasted_iota(jnp.int32, (2 * BLOCKS, BLOCKS), 0).astype(F32)
    select = jnp.where(slot == place, 1.0, 0.0).astype(BF16)
    label = jnp.broadcast_to(sub_ref[...].astype(F32), (BLOCKS, BLOCKS)).T

    pl.semaphore_wait(ready_sem, LATS - 1)

    def send_group(turn, carry):
        _, lon_to = partner(turn * LATS, lat, lon)
        first = windows[pl.ds(2 * lon_to, BLOCKS, stride=CHANS), :]
        second = windows[pl.ds(2 * lon_to + 1, BLOCKS, stride=CHANS), :]
        first = jnp.where(across == LABEL, label, first)
        both = jnp.concatenate([first.astype(BF16), second.astype(BF16)], axis=1)
        packed[turn] = jnp.dot(select, both, preferred_element_type=F32).astype(BF16)

        def send(hop, inner):
            lat_to, lon_there = partner(turn * LATS + hop, lat, lon)
            pltpu.make_async_remote_copy(
                src_ref=packed.at[turn, pl.ds(pl.multiple_of(lat_to * PAIR, PAIR), PAIR)],
                dst_ref=got.at[turn * LATS + hop],
                send_sem=send_sem,
                recv_sem=recv_sem.at[turn],
                device_id=(lat_to, lon_there),
                device_id_type=MESH,
            ).start()
            return inner

        @pl.when(turn > 0)
        def _():
            send(0, 0)

        @pl.when(turn == 0)
        def _():
            got[0] = packed[0, pl.ds(pl.multiple_of(lat * PAIR, PAIR), PAIR), :]

        lax.fori_loop(1, LATS, send, 0)
        return carry

    lax.fori_loop(0, LONS, send_group, 0)

    summed[...] = jnp.zeros_like(summed)
    wait_for(lon_raw, load_sem.at[0])

    def prepare_lon(part, carry):
        for residue in range(8):
            rows = lon_raw[part, pl.ds(residue, 256, stride=8), :]
            lon_half[part, residue * 256 : (residue + 1) * 256, :] = rows.astype(BF16)
        return carry

    lax.fori_loop(0, 16, prepare_lon, 0)
    wait_for(lat_raw, load_sem.at[1])

    def prepare_lat(part, carry):
        start = pl.multiple_of(part * 128, 128)
        for piece in range(8):
            turned = lat_raw[pl.ds(start, 128), piece * 128 : (piece + 1) * 128].T
            high = turned.astype(BF16)
            lat_high[part, piece * 128 : (piece + 1) * 128, :] = high
            lat_low[part, piece * 128 : (piece + 1) * 128, :] = (
                turned - high.astype(F32)
            ).astype(BF16)
        return carry

    lax.fori_loop(0, 8, prepare_lat, 0)

    lanes = lax.broadcasted_iota(jnp.int32, (256, 256), 1).astype(F32)
    tile = (lax.broadcasted_iota(jnp.int32, (256, 1), 0) // 2) % 8

    def add_group(turn):
        view = got.at[pl.ds(turn * LATS, LATS)]
        if turn == 0:
            wait_for(got.at[pl.ds(1, LATS - 1)], recv_sem.at[0])
        else:
            wait_for(view, recv_sem.at[turn])
        chunk = got[turn * LATS : (turn + 1) * LATS].reshape(256, 256)
        name = chunk[:, LABEL : LABEL + 1].astype(F32).astype(jnp.int32)
        goal = ((name // 32) * 256 + tile * 32 + name % 32).astype(F32)
        goal = jnp.broadcast_to(goal, (256, 256)) - lanes
        turned = chunk.astype(F32).T.astype(BF16)
        for band in range(8):
            match = jnp.where(goal == float(band * 256), 1.0, 0.0).astype(BF16)
            add = jnp.dot(turned, match, preferred_element_type=F32)
            summed[2 * band + 2, 0:256, :] += add[:, :128]
            summed[2 * band + 3, 0:256, :] += add[:, 128:]

    for turn in range(LONS):
        add_group(turn)

    tail_mask = lax.broadcasted_iota(jnp.int32, (8, 256), 0) < 3

    def fold(band, carry):
        def rows(block, start, stride):
            return jnp.concatenate(
                [
                    summed[2 * block + half, pl.ds(start, 8, stride=stride), :]
                    for half in range(2)
                ],
                axis=1,
            )

        def column(chan, v):
            main = rows(band + 1, chan * 128 + v, 16)
            if v < 10:
                over = rows(band, chan * 128 + 11 + v % 5 + 48 * (v // 5), 16)
            else:
                over = rows(band, chan * 128 + 96 + 11, 1)
            return main + jnp.where(tail_mask, over, 0.0)

        def residue_of(chan, q):
            if q == 7:
                return column(chan, 8) + pltpu.roll(column(chan, 0), 255, 1)
            if q < 2:
                return column(chan, q + 1) + pltpu.roll(column(chan, q + 9), 1, 1)
            return column(chan, q + 1)

        for q in range(8):
            value = jnp.concatenate([residue_of(0, q), residue_of(1, q)], axis=0)
            high = value.astype(BF16)
            coeff[pl.ds(pl.multiple_of(band * 16, 16), 16), q * 256 : (q + 1) * 256] = high
            coeff[pl.ds(pl.multiple_of(ROWS + band * 16, 16), 16), q * 256 : (q + 1) * 256] = (
                value - high.astype(F32)
            ).astype(BF16)
        return carry

    lax.fori_loop(0, BANDS, fold, 0)

    def line_group(step, carry):
        group = (lat // 2 + step) % 8
        weights = jnp.concatenate([lon_half[2 * group], lon_half[2 * group + 1]], axis=1)
        product = jnp.dot(coeff[...], weights, preferred_element_type=F32)
        total = (product[:ROWS] + product[ROWS:]).astype(BF16)
        for half in range(2):
            there = 2 * group + half
            lines[there] = total[:, half * 128 : (half + 1) * 128]

            @pl.when(there != lat)
            def _():
                pltpu.make_async_remote_copy(
                    src_ref=lines.at[there],
                    dst_ref=columns.at[lat],
                    send_sem=line_send,
                    recv_sem=line_recv,
                    device_id=(there, lon),
                    device_id_type=MESH,
                ).start()

        return carry

    lax.fori_loop(1, 9, line_group, 0)
    wait_for(columns.at[pl.ds(0, LATS - 1)], line_recv)
    columns[lat] = lines[lat]

    def assemble(source, carry):
        before = jnp.maximum(source - 1, 0)
        tail = columns[before, 128:144, :].astype(F32)
        for band in range(8):
            value = columns[source, band * 16 : (band + 1) * 16, :].astype(F32)
            if band == 0:
                value = value + jnp.where(source > 0, tail, 0.0)
            start = pl.multiple_of(source * 64 + band * 8, 8)
            column_sum[pl.ds(start, 8), 0:128] = value[0:8]
            column_sum[pl.ds(start, 8), 128:256] = value[8:16]
        return carry

    lax.fori_loop(0, LATS, assemble, 0)
    last = columns[LATS - 1, 128:144, :].astype(F32)
    column_sum[NLAT : NLAT + 8, 0:128] = last[0:8]
    column_sum[NLAT : NLAT + 8, 128:256] = last[8:16]
    whole = column_sum[1 : NLAT + 1, :].astype(BF16)

    for piece in range(4):
        span = slice(piece * 256, (piece + 1) * 256)
        high = jnp.concatenate([lat_high[part, span, :] for part in range(8)], axis=1)
        low_part = jnp.concatenate([lat_low[part, span, :] for part in range(8)], axis=1)
        result = jnp.dot(high, whole, preferred_element_type=F32) + jnp.dot(
            low_part, whole, preferred_element_type=F32
        )
        out_ref[0, span, :] = result[:, :128]
        out_ref[1, span, :] = result[:, 128:]

    wait_for(got.at[pl.ds(0, LATS * LONS - 1)], send_sem)
    wait_for(lines.at[pl.ds(0, LATS - 1)], line_send)


def on_device(cotangent, fractions, offsets, owner, sub_block, lon_inverse, lat_inverse):
    vmem = pl.BlockSpec(memory_space=pltpu.VMEM)
    anywhere = pl.BlockSpec(memory_space=pl.ANY)
    return pl.pallas_call(
        kernel,
        out_shape=jax.ShapeDtypeStruct((2, NLAT, 128), F32),
        in_specs=[vmem] * 5 + [anywhere] * 2,
        out_specs=vmem,
        scratch_shapes=[
            pltpu.VMEM((8, 16, 128), F32),
            pltpu.VMEM((BLOCKS * CHANS, 128), F32),
            pltpu.VMEM((LONS, 256, 256), BF16),
            pltpu.VMEM((LATS * LONS, PAIR, 256), BF16),
            pltpu.VMEM((20, 320, 128), F32),
            pltpu.VMEM((2 * ROWS, NLON), BF16),
            pltpu.VMEM((16, NLON, 128), F32),
            pltpu.VMEM((16, NLON, 128), BF16),
            pltpu.VMEM((NLAT, NLAT), F32),
            pltpu.VMEM((8, NLAT, 128), BF16),
            pltpu.VMEM((8, NLAT, 128), BF16),
            pltpu.VMEM((LATS, ROWS, 128), BF16),
            pltpu.VMEM((LATS, ROWS, 128), BF16),
            pltpu.VMEM((NLAT + 8, 256), F32),
            pltpu.SemaphoreType.REGULAR,
            pltpu.SemaphoreType.DMA((2,)),
            pltpu.SemaphoreType.DMA,
            pltpu.SemaphoreType.DMA((LONS,)),
            pltpu.SemaphoreType.DMA,
            pltpu.SemaphoreType.DMA,
        ],
        compiler_params=pltpu.CompilerParams(
            collective_id=0, has_side_effects=True, vmem_limit_bytes=60 * 2**20
        ),
    )(cotangent, fractions, offsets, owner, sub_block.reshape(1, BLOCKS), lon_inverse, lat_inverse)


def solution(mesh):
    return jax.shard_map(
        on_device,
        mesh=mesh,
        in_specs=(
            P(("lat", "lon"), None, None),
            P(("lat", "lon"), None, None),
            P(("lat", "lon"), None, None),
            P(("lat", "lon"), None),
            P(("lat", "lon")),
            P(),
            P(),
        ),
        out_specs=P("lon", None, "lat"),
        check_vma=False,
    )
```

```python
import jax
import jax.numpy as jnp
from jax import lax
from jax.experimental import pallas as pl
from jax.experimental.pallas import tpu as pltpu
from jax.sharding import PartitionSpec as P

MESH = pl.DeviceIdType.MESH
F32 = jnp.float32
BF16 = jnp.bfloat16
LATS = 16
LONS = 8
BLOCKS = 128
CHANS = 16
NLAT = 1024
NLON = 2048
PAIR = 16
LABEL = 127
BANDS = 9
ROWS = BANDS * 16


def partner(step, lat, lon):
    turn, hop = step // LATS, step % LATS
    x = (lat // 4 + hop // 4) % 4
    y = (lat % 4 + hop % 4) % 4
    z = (lon // 2 + turn // 2) % 4
    core = (lon % 2 + turn % 2) % 2
    return x * 4 + y, z * 2 + core


def spline(distance):
    size = jnp.abs(distance)
    far = jnp.maximum(2.0 - size, 0.0)
    near = jnp.maximum(1.0 - size, 0.0)
    return far * far * far - 4.0 * (near * near * near)


def wait_for(view, sem):
    pltpu.make_async_copy(view, view, sem).wait()


def sublane_places(first):
    row = lax.broadcasted_iota(jnp.int32, (8, 128), 0)
    return jnp.where(row < 3, row + 8, first(row)).astype(F32)


def kernel(cot_hbm, frac_hbm, off_hbm, owner_hbm, sub_hbm, lon_ref, lat_ref, out_ref,
           cot_ref, frac_ref, off_ref, owner_ref, sub_ref, lat_tab, windows, packed, got, summed, coeff, lon_raw, lon_half, lat_raw, lat_high,
           lat_low, lines, columns, column_sum,
           ready_sem, load_sem, send_sem, recv_sem, line_send, line_recv):
    lat, lon = lax.axis_index("lat"), lax.axis_index("lon")
    barrier = pltpu.get_barrier_semaphore()
    inputs = [
        pltpu.make_async_copy(source, target, load_sem.at[2 + place])
        for place, (source, target) in enumerate(
            (
                (cot_hbm, cot_ref),
                (frac_hbm, frac_ref),
                (off_hbm, off_ref),
                (owner_hbm, owner_ref),
                (sub_hbm, sub_ref),
            )
        )
    ]
    for copy in inputs:
        copy.start()

    def greet(step, carry):
        lat_to, lon_to = partner(step, lat, lon)
        pl.semaphore_signal(barrier, inc=1, device_id=(lat_to, lon_to), device_id_type=MESH)
        return carry

    lax.fori_loop(1, LATS, greet, 0)
    lax.fori_loop(1, LONS, lambda turn, carry: greet(turn * LATS, carry), 0)

    for part in range(16):
        pltpu.make_async_copy(
            lon_ref.at[:, pl.ds(part * 128, 128)], lon_raw.at[part], load_sem.at[0]
        ).start()
    pltpu.make_async_copy(lat_ref, lat_raw, load_sem.at[1]).start()

    for copy in inputs:
        copy.wait()

    index = lax.broadcasted_iota(jnp.int32, (8, 128), 0)
    low = index.astype(F32)
    low_tail = index < 3
    ends_a = sublane_places(lambda row: row - 3)
    ends_b = sublane_places(lambda row: row + 2)
    ends_c = sublane_places(lambda row: jnp.where(row < 6, 10, 15))
    lat_c = jnp.where(low_tail, 6, jnp.where(index < 6, index + 5, 15)).astype(F32)

    def window_group(group, carry):
        places = off_ref[pl.ds(group * 8, 8)].astype(F32) + 1.0 + frac_ref[pl.ds(group * 8, 8)]
        for item in range(8):
            block = group * 8 + item
            centre_lat = jnp.broadcast_to(places[item, 0:1, :], (8, 128))
            centre_lon = jnp.broadcast_to(places[item, 1:2, :], (8, 128))
            lat_tab[item, 0:8, :] = spline(low - centre_lat) * (1.0 / 36.0)
            lat_tab[item, 8:16, :] = spline(low + 8.0 - centre_lat) * (1.0 / 36.0)
            lat_last = spline(lat_c - centre_lat) * (1.0 / 36.0)
            lon_head = spline(low - centre_lon)
            tail_a = spline(ends_a - centre_lon)
            tail_b = spline(ends_b - centre_lon)
            tail_c = spline(ends_c - centre_lon)

            def lat_row(w):
                return jnp.broadcast_to(lat_tab[item, w : w + 1, :], (8, 128))

            high_rows = [lat_row(8), lat_row(9), lat_row(10)]
            pieces = []
            for w in range(8):
                row = lat_row(w)
                if w < 6:
                    tail_lat = jnp.where(low_tail, row, high_rows[w % 3])
                elif w == 6:
                    tail_lat = lat_last
                else:
                    tail_lat = row
                tail_lon = tail_a if w < 3 else (tail_b if w < 6 else tail_c)
                pieces.append(row * lon_head)
                pieces.append(tail_lat * tail_lon)
            stencil = jnp.concatenate(pieces, axis=0).astype(BF16)
            window = lax.dot_general(
                cot_ref[block], stencil, (((1,), (1,)), ((), ())), preferred_element_type=F32
            )
            windows[pl.ds(pl.multiple_of(block * CHANS, CHANS), CHANS), :] = window
        return carry

    lax.fori_loop(0, 12, window_group, 0)

    pl.semaphore_wait(barrier, LATS - 1 + LONS - 1)

    def tell(step, carry):
        lat_to, lon_to = partner(step, lat, lon)
        pl.semaphore_signal(ready_sem, inc=1, device_id=(lat_to, lon_to), device_id_type=MESH)
        return carry

    lax.fori_loop(1, LONS, lambda turn, carry: tell(turn * LATS, carry), 0)
    lax.fori_loop(12, 16, window_group, 0)

    own_across = jnp.broadcast_to(owner_ref[...].astype(F32), (BLOCKS, BLOCKS))
    own_down = own_across.T
    down = lax.broadcasted_iota(jnp.int32, (BLOCKS, BLOCKS), 0)
    across = lax.broadcasted_iota(jnp.int32, (BLOCKS, BLOCKS), 1)
    earlier = jnp.where((own_down == own_across) & (down < across), 1.0, 0.0)
    place = 2.0 * own_across[0:1, :] + jnp.sum(earlier, axis=0, keepdims=True)
    slot = lax.broadcasted_iota(jnp.int32, (2 * BLOCKS, BLOCKS), 0).astype(F32)
    select = jnp.where(slot == place, 1.0, 0.0).astype(BF16)
    label = jnp.broadcast_to(sub_ref[...].astype(F32), (BLOCKS, BLOCKS)).T

    def send_group(turn, carry):
        _, lon_to = partner(turn * LATS, lat, lon)
        first = windows[pl.ds(2 * lon_to, BLOCKS, stride=CHANS), :]
        second = windows[pl.ds(2 * lon_to + 1, BLOCKS, stride=CHANS), :]
        first = jnp.where(across == LABEL, label, first)
        both = jnp.concatenate([first.astype(BF16), second.astype(BF16)], axis=1)
        packed[turn] = jnp.dot(select, both, preferred_element_type=F32).astype(BF16)

        def send(hop, inner):
            lat_to, lon_there = partner(turn * LATS + hop, lat, lon)
            pltpu.make_async_remote_copy(
                src_ref=packed.at[turn, pl.ds(pl.multiple_of(lat_to * PAIR, PAIR), PAIR)],
                dst_ref=got.at[turn * LATS + hop],
                send_sem=send_sem,
                recv_sem=recv_sem.at[turn],
                device_id=(lat_to, lon_there),
                device_id_type=MESH,
            ).start()
            return inner

        if isinstance(turn, int):
            got[0] = packed[0, pl.ds(pl.multiple_of(lat * PAIR, PAIR), PAIR), :]
            lax.fori_loop(1, LATS, send, 0)
        else:
            lax.fori_loop(0, LATS, send, 0)
        return carry

    send_group(0, 0)
    pl.semaphore_wait(ready_sem, LONS - 1)
    lax.fori_loop(1, LONS, send_group, 0)

    summed[...] = jnp.zeros_like(summed)
    wait_for(lon_raw, load_sem.at[0])

    def prepare_lon(part, carry):
        for residue in range(8):
            rows = lon_raw[part, pl.ds(residue, 256, stride=8), :]
            lon_half[part, residue * 256 : (residue + 1) * 256, :] = rows.astype(BF16)
        return carry

    lax.fori_loop(0, 16, prepare_lon, 0)
    wait_for(lat_raw, load_sem.at[1])

    def prepare_lat(part, carry):
        start = pl.multiple_of(part * 128, 128)
        for piece in range(8):
            turned = lat_raw[pl.ds(start, 128), piece * 128 : (piece + 1) * 128].T
            high = turned.astype(BF16)
            lat_high[part, piece * 128 : (piece + 1) * 128, :] = high
            lat_low[part, piece * 128 : (piece + 1) * 128, :] = (
                turned - high.astype(F32)
            ).astype(BF16)
        return carry

    lax.fori_loop(0, 8, prepare_lat, 0)

    lanes = lax.broadcasted_iota(jnp.int32, (256, 256), 1).astype(F32)
    tile = (lax.broadcasted_iota(jnp.int32, (256, 1), 0) // 2) % 8

    def add_group(turn):
        view = got.at[pl.ds(turn * LATS, LATS)]
        if turn == 0:
            wait_for(got.at[pl.ds(1, LATS - 1)], recv_sem.at[0])
        else:
            wait_for(view, recv_sem.at[turn])
        chunk = got[turn * LATS : (turn + 1) * LATS].reshape(256, 256)
        name = chunk[:, LABEL : LABEL + 1].astype(F32).astype(jnp.int32)
        goal = ((name // 32) * 256 + tile * 32 + name % 32).astype(F32)
        goal = jnp.broadcast_to(goal, (256, 256)) - lanes
        turned = chunk.astype(F32).T.astype(BF16)
        for band in range(8):
            match = jnp.where(goal == float(band * 256), 1.0, 0.0).astype(BF16)
            add = jnp.dot(turned, match, preferred_element_type=F32)
            summed[2 * band + 2, 0:256, :] += add[:, :128]
            summed[2 * band + 3, 0:256, :] += add[:, 128:]

    for turn in range(LONS):
        add_group(turn)

    tail_mask = lax.broadcasted_iota(jnp.int32, (8, 256), 0) < 3

    def fold(band, carry):
        def rows(block, start, stride):
            return jnp.concatenate(
                [
                    summed[2 * block + half, pl.ds(start, 8, stride=stride), :]
                    for half in range(2)
                ],
                axis=1,
            )

        def column(chan, v):
            main = rows(band + 1, chan * 128 + v, 16)
            if v < 10:
                over = rows(band, chan * 128 + 11 + v % 5 + 48 * (v // 5), 16)
            else:
                over = rows(band, chan * 128 + 96 + 11, 1)
            return main + jnp.where(tail_mask, over, 0.0)

        def residue_of(chan, q):
            if q == 7:
                return column(chan, 8) + pltpu.roll(column(chan, 0), 255, 1)
            if q < 2:
                return column(chan, q + 1) + pltpu.roll(column(chan, q + 9), 1, 1)
            return column(chan, q + 1)

        for q in range(8):
            value = jnp.concatenate([residue_of(0, q), residue_of(1, q)], axis=0)
            high = value.astype(BF16)
            coeff[pl.ds(pl.multiple_of(band * 16, 16), 16), q * 256 : (q + 1) * 256] = high
            coeff[pl.ds(pl.multiple_of(ROWS + band * 16, 16), 16), q * 256 : (q + 1) * 256] = (
                value - high.astype(F32)
            ).astype(BF16)
        return carry

    lax.fori_loop(0, BANDS, fold, 0)

    def line_group(step, carry):
        group = (lat // 2 + step) % 8
        weights = jnp.concatenate([lon_half[2 * group], lon_half[2 * group + 1]], axis=1)
        product = jnp.dot(coeff[...], weights, preferred_element_type=F32)
        total = (product[:ROWS] + product[ROWS:]).astype(BF16)
        for half in range(2):
            there = 2 * group + half
            lines[there] = total[:, half * 128 : (half + 1) * 128]

            @pl.when(there != lat)
            def _():
                pltpu.make_async_remote_copy(
                    src_ref=lines.at[there],
                    dst_ref=columns.at[lat],
                    send_sem=line_send,
                    recv_sem=line_recv,
                    device_id=(there, lon),
                    device_id_type=MESH,
                ).start()

        return carry

    lax.fori_loop(1, 9, line_group, 0)
    wait_for(columns.at[pl.ds(0, LATS - 1)], line_recv)
    columns[lat] = lines[lat]

    def assemble(source, carry):
        before = jnp.maximum(source - 1, 0)
        tail = columns[before, 128:144, :].astype(F32)
        for band in range(8):
            value = columns[source, band * 16 : (band + 1) * 16, :].astype(F32)
            if band == 0:
                value = value + jnp.where(source > 0, tail, 0.0)
            start = pl.multiple_of(source * 64 + band * 8, 8)
            column_sum[pl.ds(start, 8), 0:128] = value[0:8]
            column_sum[pl.ds(start, 8), 128:256] = value[8:16]
        return carry

    lax.fori_loop(0, LATS, assemble, 0)
    last = columns[LATS - 1, 128:144, :].astype(F32)
    column_sum[NLAT : NLAT + 8, 0:128] = last[0:8]
    column_sum[NLAT : NLAT + 8, 128:256] = last[8:16]
    whole = column_sum[1 : NLAT + 1, :].astype(BF16)

    for piece in range(4):
        span = slice(piece * 256, (piece + 1) * 256)
        high = jnp.concatenate([lat_high[part, span, :] for part in range(8)], axis=1)
        low_part = jnp.concatenate([lat_low[part, span, :] for part in range(8)], axis=1)
        result = jnp.dot(high, whole, preferred_element_type=F32) + jnp.dot(
            low_part, whole, preferred_element_type=F32
        )
        out_ref[0, span, :] = result[:, :128]
        out_ref[1, span, :] = result[:, 128:]

    wait_for(got.at[pl.ds(0, LATS * LONS - 1)], send_sem)
    wait_for(lines.at[pl.ds(0, LATS - 1)], line_send)


def on_device(cotangent, fractions, offsets, owner, sub_block, lon_inverse, lat_inverse):
    vmem = pl.BlockSpec(memory_space=pltpu.VMEM)
    hbm = pl.BlockSpec(memory_space=pltpu.HBM)
    operands = (
        cotangent, fractions, offsets, owner.reshape(1, BLOCKS), sub_block.reshape(1, BLOCKS),
        lon_inverse, lat_inverse,
    )
    return pl.pallas_call(
        kernel,
        out_shape=jax.ShapeDtypeStruct((2, NLAT, 128), F32),
        in_specs=[hbm] * 7,
        out_specs=vmem,
        scratch_shapes=[
            pltpu.VMEM((BLOCKS, CHANS, 128), BF16),
            pltpu.VMEM((BLOCKS, 2, 128), F32),
            pltpu.VMEM((BLOCKS, 2, 128), jnp.int32),
            pltpu.VMEM((1, BLOCKS), jnp.int32),
            pltpu.VMEM((1, BLOCKS), jnp.int32),
            pltpu.VMEM((8, 16, 128), F32),
            pltpu.VMEM((BLOCKS * CHANS, 128), F32),
            pltpu.VMEM((LONS, 256, 256), BF16),
            pltpu.VMEM((LATS * LONS, PAIR, 256), BF16),
            pltpu.VMEM((20, 320, 128), F32),
            pltpu.VMEM((2 * ROWS, NLON), BF16),
            pltpu.VMEM((16, NLON, 128), F32),
            pltpu.VMEM((16, NLON, 128), BF16),
            pltpu.VMEM((NLAT, NLAT), F32),
            pltpu.VMEM((8, NLAT, 128), BF16),
            pltpu.VMEM((8, NLAT, 128), BF16),
            pltpu.VMEM((LATS, ROWS, 128), BF16),
            pltpu.VMEM((LATS, ROWS, 128), BF16),
            pltpu.VMEM((NLAT + 8, 256), F32),
            pltpu.SemaphoreType.REGULAR,
            pltpu.SemaphoreType.DMA((7,)),
            pltpu.SemaphoreType.DMA,
            pltpu.SemaphoreType.DMA((LONS,)),
            pltpu.SemaphoreType.DMA,
            pltpu.SemaphoreType.DMA,
        ],
        compiler_params=pltpu.CompilerParams(
            collective_id=0, has_side_effects=True, vmem_limit_bytes=50 * 2**20
        ),
    )(*(pltpu.with_memory_space_constraint(value, pltpu.HBM) for value in operands))


def solution(mesh):
    return jax.shard_map(
        on_device,
        mesh=mesh,
        in_specs=(
            P(("lat", "lon"), None, None),
            P(("lat", "lon"), None, None),
            P(("lat", "lon"), None, None),
            P(("lat", "lon"), None),
            P(("lat", "lon")),
            P(),
            P(),
        ),
        out_specs=P("lon", None, "lat"),
        check_vma=False,
    )
```

```python
import jax
import jax.numpy as jnp
from jax import lax
from jax.experimental import pallas as pl
from jax.experimental.pallas import tpu as pltpu
from jax.sharding import PartitionSpec as P

MESH = pl.DeviceIdType.MESH
F32 = jnp.float32
BF16 = jnp.bfloat16
LATS = 16
LONS = 8
BLOCKS = 128
CHANS = 16
NLAT = 1024
NLON = 2048
PAIR = 16
LABEL = 127
ROWS = 80
SELF = 8
STEPS = LATS * LONS


def spline(distance):
    size = jnp.abs(distance)
    far = jnp.maximum(2.0 - size, 0.0)
    near = jnp.maximum(1.0 - size, 0.0)
    return far * far * far - 4.0 * (near * near * near)


def wait_for(view, sem):
    pltpu.make_async_copy(view, view, sem).wait()


def sublane_places(first):
    row = lax.broadcasted_iota(jnp.int32, (8, 128), 0)
    return jnp.where(row < 3, row + 8, first(row)).astype(F32)


def kernel(cot_hbm, frac_hbm, off_hbm, owner_hbm, sub_hbm, lon_ref, lat_ref, out_ref,
           cot_ref, frac_ref, off_ref, owner_ref, sub_ref, lat_tab, windows, packed, got, summed, coeff, lon_raw, lon_half, lat_raw, lat_high,
           lat_low, lines, columns, column_sum,
           ready_sem, load_sem, send_sem, recv_sem, line_send, line_recv):
    lat, lon = lax.axis_index("lat"), lax.axis_index("lon")
    barrier = pltpu.get_barrier_semaphore()
    inputs = [
        pltpu.make_async_copy(source, target, load_sem.at[2 + place])
        for place, (source, target) in enumerate(
            (
                (cot_hbm, cot_ref),
                (frac_hbm, frac_ref),
                (off_hbm, off_ref),
                (owner_hbm, owner_ref),
                (sub_hbm, sub_ref),
            )
        )
    ]
    for copy in inputs:
        copy.start()

    lat_others = [
        (lat // 4 + dx) % 4 * 4 + (lat % 4 + dy) % 4
        for dx in range(4)
        for dy in range(4)
        if dx + dy > 0
    ]
    lon_there = [(lon // 2 + turn // 2) % 4 * 2 + (lon % 2 + turn % 2) % 2 for turn in range(8)]

    def greet(sem, lat_to, lon_to):
        pl.semaphore_signal(sem, inc=1, device_id=(lat_to, lon_to), device_id_type=MESH)

    for lat_to in lat_others:
        greet(barrier, lat_to, lon)
    for lon_to in lon_there[1:]:
        greet(barrier, lat, lon_to)

    for part in range(16):
        pltpu.make_async_copy(
            lon_ref.at[:, pl.ds(part * 128, 128)], lon_raw.at[part], load_sem.at[0]
        ).start()
    pltpu.make_async_copy(lat_ref, lat_raw, load_sem.at[1]).start()

    for copy in inputs:
        copy.wait()

    index = lax.broadcasted_iota(jnp.int32, (8, 128), 0)
    low = index.astype(F32)
    low_tail = index < 3
    ends_a = sublane_places(lambda row: row - 3)
    ends_b = sublane_places(lambda row: row + 2)
    ends_c = sublane_places(lambda row: jnp.where(row < 6, 10, 15))
    lat_c = jnp.where(low_tail, 6, jnp.where(index < 6, index + 5, 15)).astype(F32)

    def window_group(group, carry):
        places = off_ref[pl.ds(group * 8, 8)].astype(F32) + 1.0 + frac_ref[pl.ds(group * 8, 8)]
        for item in range(8):
            block = group * 8 + item
            centre_lat = jnp.broadcast_to(places[item, 0:1, :], (8, 128))
            centre_lon = jnp.broadcast_to(places[item, 1:2, :], (8, 128))
            lat_tab[item, 0:8, :] = spline(low - centre_lat) * (1.0 / 36.0)
            lat_tab[item, 8:16, :] = spline(low + 8.0 - centre_lat) * (1.0 / 36.0)
            lat_last = spline(lat_c - centre_lat) * (1.0 / 36.0)
            lon_head = spline(low - centre_lon)
            tail_a = spline(ends_a - centre_lon)
            tail_b = spline(ends_b - centre_lon)
            tail_c = spline(ends_c - centre_lon)

            def lat_row(w):
                return jnp.broadcast_to(lat_tab[item, w : w + 1, :], (8, 128))

            high_rows = [lat_row(8), lat_row(9), lat_row(10)]
            pieces = []
            for w in range(8):
                row = lat_row(w)
                if w < 6:
                    tail_lat = jnp.where(low_tail, row, high_rows[w % 3])
                elif w == 6:
                    tail_lat = lat_last
                else:
                    tail_lat = row
                tail_lon = tail_a if w < 3 else (tail_b if w < 6 else tail_c)
                pieces.append(row * lon_head)
                pieces.append(tail_lat * tail_lon)
            stencil = jnp.concatenate(pieces, axis=0).astype(BF16)
            window = lax.dot_general(
                cot_ref[block], stencil, (((1,), (1,)), ((), ())), preferred_element_type=F32
            )
            windows[pl.ds(pl.multiple_of(block * CHANS, CHANS), CHANS), :] = window
        return carry

    lax.fori_loop(0, 12, window_group, 0)

    pl.semaphore_wait(barrier, LATS - 1 + LONS - 1)

    for lon_to in lon_there[1:]:
        greet(ready_sem, lat, lon_to)
    lax.fori_loop(12, 16, window_group, 0)

    own_across = jnp.broadcast_to(owner_ref[...].astype(F32), (BLOCKS, BLOCKS))
    own_down = own_across.T
    down = lax.broadcasted_iota(jnp.int32, (BLOCKS, BLOCKS), 0)
    across = lax.broadcasted_iota(jnp.int32, (BLOCKS, BLOCKS), 1)
    earlier = jnp.where((own_down == own_across) & (down < across), 1.0, 0.0)
    place = 2.0 * own_across[0:1, :] + jnp.sum(earlier, axis=0, keepdims=True)
    slot = lax.broadcasted_iota(jnp.int32, (2 * BLOCKS, BLOCKS), 0).astype(F32)
    select = jnp.where(slot == place, 1.0, 0.0).astype(BF16)
    label = jnp.broadcast_to(sub_ref[...].astype(F32), (BLOCKS, BLOCKS)).T

    def pack(chan):
        for pair in range(0, LONS, 2):
            sides = []
            for lon_to in (pair, pair + 1):
                window = windows[pl.ds(2 * lon_to + chan, BLOCKS, stride=CHANS), :]
                sides.append(jnp.where(across == LABEL, label, window).astype(BF16))
            both = jnp.concatenate(sides, axis=1)
            slots = jnp.dot(select, both, preferred_element_type=F32).astype(BF16)
            packed[chan, pair] = slots[:, :128]
            packed[chan, pair + 1] = slots[:, 128:]
        start = pl.multiple_of(lat * PAIR, PAIR)
        got[chan, SELF] = packed[chan, lon, pl.ds(start, PAIR), :]

    def send_group(chan):
        def body(group, carry):
            for half in range(2):
                x = (lat // 4 + group // 4 + 2 - 2 * half) % 4
                y = (lat % 4 + group % 4 + 2 - 2 * half) % 4
                lat_to = x * 4 + y
                start = pl.multiple_of(lat_to * PAIR, PAIR)
                for turn in range(8):
                    step = group * 16 + half * 8 + turn
                    copy = pltpu.make_async_remote_copy(
                        src_ref=packed.at[chan, lon_there[turn], pl.ds(start, PAIR)],
                        dst_ref=got.at[chan, step],
                        send_sem=send_sem.at[chan],
                        recv_sem=recv_sem.at[chan * 8 + group],
                        device_id=(lat_to, lon_there[turn]),
                        device_id_type=MESH,
                    )
                    if half * 8 + turn == SELF:
                        pl.when(group > 0)(copy.start)
                    else:
                        copy.start()
            return carry

        return body

    pack(0)
    pl.semaphore_wait(ready_sem, LONS - 1)
    lax.fori_loop(0, 8, send_group(0), 0)
    pack(1)

    wait_for(lon_raw, load_sem.at[0])

    def prepare_lon(part, carry):
        for residue in range(8):
            rows = lon_raw[part, pl.ds(residue, 256, stride=8), :]
            lon_half[part, residue * 256 : (residue + 1) * 256, :] = rows.astype(BF16)
        return carry

    lax.fori_loop(0, 16, prepare_lon, 0)
    summed[...] = jnp.zeros_like(summed)

    def prepare_lat(part, carry):
        start = pl.multiple_of(part * 128, 128)
        for piece in range(8):
            turned = lat_raw[pl.ds(start, 128), piece * 128 : (piece + 1) * 128].T
            high = turned.astype(BF16)
            lat_high[part, piece * 128 : (piece + 1) * 128, :] = high
            lat_low[part, piece * 128 : (piece + 1) * 128, :] = (
                turned - high.astype(F32)
            ).astype(BF16)
        return carry

    lanes = lax.broadcasted_iota(jnp.int32, (256, 256), 1).astype(F32)
    tile = (lax.broadcasted_iota(jnp.int32, (256, 1), 0) // 2) % 8

    def add_group(chan, group):
        if group == 0:
            wait_for(got.at[chan, pl.ds(0, 15)], recv_sem.at[chan * 8])
        else:
            wait_for(got.at[chan, pl.ds(group * 16, 16)], recv_sem.at[chan * 8 + group])
        chunk = got[chan, group * 16 : (group + 1) * 16].reshape(256, 128)
        name = chunk[:, LABEL : LABEL + 1].astype(F32).astype(jnp.int32)
        goal = ((name // 32) * 256 + tile * 32 + name % 32).astype(F32)
        goal = jnp.broadcast_to(goal, (256, 256)) - lanes
        turned = chunk.astype(F32).T.astype(BF16)
        for band in range(8):
            match = jnp.where(goal == float(band * 256), 1.0, 0.0).astype(BF16)
            add = jnp.dot(turned, match, preferred_element_type=F32)
            summed[chan, 2 * band + 2, 0:128, :] += add[:, :128]
            summed[chan, 2 * band + 3, 0:128, :] += add[:, 128:]

    tail_mask = lax.broadcasted_iota(jnp.int32, (8, 256), 0) < 3

    def fold(chan):
        def rows(block, start, stride):
            return jnp.concatenate(
                [
                    summed[chan, 2 * block + half, pl.ds(start, 8, stride=stride), :]
                    for half in range(2)
                ],
                axis=1,
            )

        def fold_pair(pair, carry):
            def column(band, v):
                main = rows(band + 1, v, 16)
                if v < 10:
                    over = rows(band, 11 + v % 5 + 48 * (v // 5), 16)
                else:
                    over = rows(band, 96 + 11, 1)
                return main + jnp.where(tail_mask, over, 0.0)

            def residue_of(band, q):
                if q == 7:
                    return column(band, 8) + pltpu.roll(column(band, 0), 255, 1)
                if q < 2:
                    return column(band, q + 1) + pltpu.roll(column(band, q + 9), 1, 1)
                return column(band, q + 1)

            for q in range(8):
                value = jnp.concatenate(
                    [residue_of(2 * pair, q), residue_of(2 * pair + 1, q)], axis=0
                )
                high = value.astype(BF16)
                span = slice(q * 256, (q + 1) * 256)
                coeff[chan, pl.ds(pl.multiple_of(pair * 16, 16), 16), span] = high
                coeff[chan, pl.ds(pl.multiple_of(ROWS + pair * 16, 16), 16), span] = (
                    value - high.astype(F32)
                ).astype(BF16)
            return carry

        lax.fori_loop(0, 5, fold_pair, 0)

    def send_lines(chan):
        def line_group(step, carry):
            group = (lat // 2 + step) % 8
            weights = jnp.concatenate([lon_half[2 * group], lon_half[2 * group + 1]], axis=1)
            product = jnp.dot(coeff[chan], weights, preferred_element_type=F32)
            total = (product[:ROWS] + product[ROWS:]).astype(BF16)
            for half in range(2):
                there = 2 * group + half
                lines[chan, there] = total[:, half * 128 : (half + 1) * 128]

                @pl.when(there != lat)
                def _():
                    pltpu.make_async_remote_copy(
                        src_ref=lines.at[chan, there],
                        dst_ref=columns.at[chan, lat],
                        send_sem=line_send.at[chan],
                        recv_sem=line_recv.at[chan],
                        device_id=(there, lon),
                        device_id_type=MESH,
                    ).start()

            return carry

        lax.fori_loop(1, 9, line_group, 0, unroll=2)

    def finish(chan):
        wait_for(columns.at[chan, pl.ds(0, LATS - 1)], line_recv.at[chan])
        columns[chan, lat] = lines[chan, lat]

        def assemble(source, carry):
            before = jnp.maximum(source - 1, 0)
            tail = columns[chan, before, 64:80, :].astype(F32)[0:8]
            for pair in range(4):
                value = columns[chan, source, pair * 16 : (pair + 1) * 16, :].astype(F32)
                start = pl.multiple_of(source * 64 + pair * 16, 16)
                if pair == 0:
                    column_sum[pl.ds(start, 8), :] = value[0:8] + jnp.where(source > 0, tail, 0.0)
                    column_sum[pl.ds(start + 8, 8), :] = value[8:16]
                else:
                    column_sum[pl.ds(start, 16), :] = value
            return carry

        lax.fori_loop(0, LATS, assemble, 0)
        column_sum[NLAT : NLAT + 8, :] = columns[chan, LATS - 1, 64:80, :].astype(F32)[0:8]
        whole = column_sum[1 : NLAT + 1, :].astype(BF16)
        for piece in range(4):
            span = slice(piece * 256, (piece + 1) * 256)
            high = jnp.concatenate([lat_high[part, span, :] for part in range(8)], axis=1)
            low_part = jnp.concatenate([lat_low[part, span, :] for part in range(8)], axis=1)
            out_ref[chan, span, :] = jnp.dot(high, whole, preferred_element_type=F32) + jnp.dot(
                low_part, whole, preferred_element_type=F32
            )

    wait_for(lat_raw, load_sem.at[1])
    lax.fori_loop(0, 8, prepare_lat, 0)
    lax.fori_loop(0, 8, send_group(1), 0)
    for group in range(8):
        add_group(0, group)
    fold(0)
    send_lines(0)
    for group in range(8):
        add_group(1, group)
    fold(1)
    send_lines(1)
    finish(0)
    finish(1)

    for chan in range(2):
        wait_for(got.at[chan, pl.ds(0, STEPS - 1)], send_sem.at[chan])
        wait_for(lines.at[chan, pl.ds(0, LATS - 1)], line_send.at[chan])


def on_device(cotangent, fractions, offsets, owner, sub_block, lon_inverse, lat_inverse):
    vmem = pl.BlockSpec(memory_space=pltpu.VMEM)
    hbm = pl.BlockSpec(memory_space=pltpu.HBM)
    operands = (
        cotangent, fractions, offsets, owner.reshape(1, BLOCKS), sub_block.reshape(1, BLOCKS),
        lon_inverse, lat_inverse,
    )
    return pl.pallas_call(
        kernel,
        out_shape=jax.ShapeDtypeStruct((2, NLAT, 128), F32),
        in_specs=[hbm] * 7,
        out_specs=vmem,
        scratch_shapes=[
            pltpu.VMEM((BLOCKS, CHANS, 128), BF16),
            pltpu.VMEM((BLOCKS, 2, 128), F32),
            pltpu.VMEM((BLOCKS, 2, 128), jnp.int32),
            pltpu.VMEM((1, BLOCKS), jnp.int32),
            pltpu.VMEM((1, BLOCKS), jnp.int32),
            pltpu.VMEM((8, 16, 128), F32),
            pltpu.VMEM((BLOCKS * CHANS, 128), F32),
            pltpu.VMEM((2, LONS, 256, 128), BF16),
            pltpu.VMEM((2, STEPS, PAIR, 128), BF16),
            pltpu.VMEM((2, 22, 176, 128), F32),
            pltpu.VMEM((2, 2 * ROWS, NLON), BF16),
            pltpu.VMEM((16, NLON, 128), F32),
            pltpu.VMEM((16, NLON, 128), BF16),
            pltpu.VMEM((NLAT, NLAT), F32),
            pltpu.VMEM((8, NLAT, 128), BF16),
            pltpu.VMEM((8, NLAT, 128), BF16),
            pltpu.VMEM((2, LATS, ROWS, 128), BF16),
            pltpu.VMEM((2, LATS, ROWS, 128), BF16),
            pltpu.VMEM((NLAT + 8, 128), F32),
            pltpu.SemaphoreType.REGULAR,
            pltpu.SemaphoreType.DMA((7,)),
            pltpu.SemaphoreType.DMA((2,)),
            pltpu.SemaphoreType.DMA((16,)),
            pltpu.SemaphoreType.DMA((2,)),
            pltpu.SemaphoreType.DMA((2,)),
        ],
        compiler_params=pltpu.CompilerParams(
            collective_id=0, has_side_effects=True, vmem_limit_bytes=50 * 2**20
        ),
    )(*(pltpu.with_memory_space_constraint(value, pltpu.HBM) for value in operands))


def solution(mesh):
    return jax.shard_map(
        on_device,
        mesh=mesh,
        in_specs=(
            P(("lat", "lon"), None, None),
            P(("lat", "lon"), None, None),
            P(("lat", "lon"), None, None),
            P(("lat", "lon"), None),
            P(("lat", "lon")),
            P(),
            P(),
        ),
        out_specs=P("lon", None, "lat"),
        check_vma=False,
    )
```

```python
import jax
import jax.numpy as jnp
from jax import lax
from jax.experimental import pallas as pl
from jax.experimental.pallas import tpu as pltpu
from jax.sharding import PartitionSpec as P

MESH = pl.DeviceIdType.MESH
F32 = jnp.float32
BF16 = jnp.bfloat16
LATS = 16
LONS = 8
BLOCKS = 128
CHANS = 16
NLAT = 1024
NLON = 2048
PAIR = 16
LABEL = 127
ROWS = 80
SELF = 8
STEPS = LATS * LONS


def spline(distance):
    size = jnp.abs(distance)
    far = jnp.maximum(2.0 - size, 0.0)
    near = jnp.maximum(1.0 - size, 0.0)
    return far * far * far - 4.0 * (near * near * near)


def wait_for(view, sem):
    pltpu.make_async_copy(view, view, sem).wait()


def sublane_places(first):
    row = lax.broadcasted_iota(jnp.int32, (8, 128), 0)
    return jnp.where(row < 3, row + 8, first(row)).astype(F32)


def kernel(cot_hbm, frac_hbm, off_hbm, owner_hbm, sub_hbm, lon_ref, lat_ref, out_ref,
           cot_ref, frac_ref, off_ref, owner_ref, sub_ref, lat_tab, windows, packed, got, summed, coeff, lon_raw, lon_half, lat_raw, lat_high,
           lat_low, lines, columns, column_sum,
           ready_sem, load_sem, send_sem, recv_sem, line_send, line_recv):
    lat, lon = lax.axis_index("lat"), lax.axis_index("lon")
    barrier = pltpu.get_barrier_semaphore()
    inputs = [
        pltpu.make_async_copy(source, target, load_sem.at[2 + place])
        for place, (source, target) in enumerate(
            (
                (cot_hbm, cot_ref),
                (frac_hbm, frac_ref),
                (off_hbm, off_ref),
                (owner_hbm, owner_ref),
                (sub_hbm, sub_ref),
            )
        )
    ]
    for copy in inputs:
        copy.start()

    lat_others = [
        (lat // 4 + dx) % 4 * 4 + (lat % 4 + dy) % 4
        for dx in range(4)
        for dy in range(4)
        if dx + dy > 0
    ]
    lon_there = [(lon // 2 + turn // 2) % 4 * 2 + (lon % 2 + turn % 2) % 2 for turn in range(8)]

    def greet(sem, lat_to, lon_to):
        pl.semaphore_signal(sem, inc=1, device_id=(lat_to, lon_to), device_id_type=MESH)

    for lat_to in lat_others:
        greet(barrier, lat_to, lon)
    for lon_to in lon_there[1:]:
        greet(barrier, lat, lon_to)

    for part in range(16):
        pltpu.make_async_copy(
            lon_ref.at[:, pl.ds(part * 128, 128)], lon_raw.at[part], load_sem.at[0]
        ).start()
    pltpu.make_async_copy(lat_ref, lat_raw, load_sem.at[1]).start()

    for copy in inputs:
        copy.wait()

    index = lax.broadcasted_iota(jnp.int32, (8, 128), 0)
    low = index.astype(F32)
    low_tail = index < 3
    ends_a = sublane_places(lambda row: row - 3)
    ends_b = sublane_places(lambda row: row + 2)
    ends_c = sublane_places(lambda row: jnp.where(row < 6, 10, 15))
    lat_c = jnp.where(low_tail, 6, jnp.where(index < 6, index + 5, 15)).astype(F32)

    def window_group(group, carry):
        places = off_ref[pl.ds(group * 8, 8)].astype(F32) + 1.0 + frac_ref[pl.ds(group * 8, 8)]
        for item in range(8):
            block = group * 8 + item
            centre_lat = jnp.broadcast_to(places[item, 0:1, :], (8, 128))
            centre_lon = jnp.broadcast_to(places[item, 1:2, :], (8, 128))
            lat_tab[item, 0:8, :] = spline(low - centre_lat) * (1.0 / 36.0)
            lat_tab[item, 8:16, :] = spline(low + 8.0 - centre_lat) * (1.0 / 36.0)
            lat_last = spline(lat_c - centre_lat) * (1.0 / 36.0)
            lon_head = spline(low - centre_lon)
            tail_a = spline(ends_a - centre_lon)
            tail_b = spline(ends_b - centre_lon)
            tail_c = spline(ends_c - centre_lon)

            def lat_row(w):
                return jnp.broadcast_to(lat_tab[item, w : w + 1, :], (8, 128))

            high_rows = [lat_row(8), lat_row(9), lat_row(10)]
            pieces = []
            for w in range(8):
                row = lat_row(w)
                if w < 6:
                    tail_lat = jnp.where(low_tail, row, high_rows[w % 3])
                elif w == 6:
                    tail_lat = lat_last
                else:
                    tail_lat = row
                tail_lon = tail_a if w < 3 else (tail_b if w < 6 else tail_c)
                pieces.append(row * lon_head)
                pieces.append(tail_lat * tail_lon)
            stencil = jnp.concatenate(pieces, axis=0).astype(BF16)
            window = lax.dot_general(
                cot_ref[block], stencil, (((1,), (1,)), ((), ())), preferred_element_type=F32
            )
            windows[pl.ds(pl.multiple_of(block * CHANS, CHANS), CHANS), :] = window
        return carry

    lax.fori_loop(0, 12, window_group, 0)

    pl.semaphore_wait(barrier, LATS - 1 + LONS - 1)

    for lon_to in lon_there[1:]:
        greet(ready_sem, lat, lon_to)
    lax.fori_loop(12, 16, window_group, 0)

    own_across = jnp.broadcast_to(owner_ref[...].astype(F32), (BLOCKS, BLOCKS))
    own_down = own_across.T
    down = lax.broadcasted_iota(jnp.int32, (BLOCKS, BLOCKS), 0)
    across = lax.broadcasted_iota(jnp.int32, (BLOCKS, BLOCKS), 1)
    earlier = jnp.where((own_down == own_across) & (down < across), 1.0, 0.0)
    place = 2.0 * own_across[0:1, :] + jnp.sum(earlier, axis=0, keepdims=True)
    slot = lax.broadcasted_iota(jnp.int32, (2 * BLOCKS, BLOCKS), 0).astype(F32)
    select = jnp.where(slot == place, 1.0, 0.0).astype(BF16)
    label = jnp.broadcast_to(sub_ref[...].astype(F32), (BLOCKS, BLOCKS)).T

    def pack(chan):
        for pair in range(0, LONS, 2):
            sides = []
            for lon_to in (pair, pair + 1):
                window = windows[pl.ds(2 * lon_to + chan, BLOCKS, stride=CHANS), :]
                sides.append(jnp.where(across == LABEL, label, window).astype(BF16))
            both = jnp.concatenate(sides, axis=1)
            slots = jnp.dot(select, both, preferred_element_type=F32).astype(BF16)
            packed[chan, pair] = slots[:, :128]
            packed[chan, pair + 1] = slots[:, 128:]
        start = pl.multiple_of(lat * PAIR, PAIR)
        got[chan, SELF] = packed[chan, lon, pl.ds(start, PAIR), :]

    def send_group(chan):
        def body(group, carry):
            for half in range(2):
                x = (lat // 4 + group // 4 + 2 - 2 * half) % 4
                y = (lat % 4 + group % 4 + 2 - 2 * half) % 4
                lat_to = x * 4 + y
                start = pl.multiple_of(lat_to * PAIR, PAIR)
                for turn in range(8):
                    step = group * 16 + half * 8 + turn
                    copy = pltpu.make_async_remote_copy(
                        src_ref=packed.at[chan, lon_there[turn], pl.ds(start, PAIR)],
                        dst_ref=got.at[chan, step],
                        send_sem=send_sem.at[chan],
                        recv_sem=recv_sem.at[chan * 8 + group],
                        device_id=(lat_to, lon_there[turn]),
                        device_id_type=MESH,
                    )
                    if half * 8 + turn == SELF:
                        pl.when(group > 0)(copy.start)
                    else:
                        copy.start()
            return carry

        return body

    pack(0)
    pl.semaphore_wait(ready_sem, LONS - 1)
    lax.fori_loop(0, 8, send_group(0), 0)
    pack(1)

    wait_for(lon_raw, load_sem.at[0])

    def prepare_lon(part, carry):
        for residue in range(8):
            rows = lon_raw[part, pl.ds(residue, 256, stride=8), :]
            lon_half[part, residue * 256 : (residue + 1) * 256, :] = rows.astype(BF16)
        return carry

    lax.fori_loop(0, 16, prepare_lon, 0)
    summed[...] = jnp.zeros_like(summed)

    def prepare_lat(part, carry):
        start = pl.multiple_of(part * 128, 128)
        for piece in range(8):
            turned = lat_raw[pl.ds(start, 128), piece * 128 : (piece + 1) * 128].T
            high = turned.astype(BF16)
            lat_high[part, piece * 128 : (piece + 1) * 128, :] = high
            lat_low[part, piece * 128 : (piece + 1) * 128, :] = (
                turned - high.astype(F32)
            ).astype(BF16)
        return carry

    lanes = lax.broadcasted_iota(jnp.int32, (256, 256), 1).astype(F32)
    tile = (lax.broadcasted_iota(jnp.int32, (256, 1), 0) // 2) % 4

    def add_group(chan, group):
        first = 32 * group
        if group == 0:
            wait_for(got.at[chan, pl.ds(0, 15)], recv_sem.at[chan * 8])
        else:
            wait_for(got.at[chan, pl.ds(first, 16)], recv_sem.at[chan * 8 + 2 * group])
        wait_for(got.at[chan, pl.ds(first + 16, 16)], recv_sem.at[chan * 8 + 2 * group + 1])
        chunk = got[chan, first : first + 32].astype(F32)
        for half in range(2):
            part = chunk[:, 8 * half : 8 * half + 8, :].reshape(256, 128)
            name = part[:, LABEL : LABEL + 1].astype(jnp.int32)
            goal = ((name // 32) * 128 + tile * 32 + name % 32).astype(F32)
            goal = jnp.broadcast_to(goal, (256, 256)) - lanes
            turned = part.T.astype(BF16)
            for pair in range(4):
                match = jnp.where(goal == float(pair * 256), 1.0, 0.0).astype(BF16)
                add = jnp.dot(turned, match, preferred_element_type=F32)
                summed[chan, 4 * pair + 2 + half, 0:128, :] += add[:, :128]
                summed[chan, 4 * pair + 4 + half, 0:128, :] += add[:, 128:]

    tail_mask = lax.broadcasted_iota(jnp.int32, (8, 256), 0) < 3

    def fold(chan):
        def rows(block, start, stride):
            return jnp.concatenate(
                [
                    summed[chan, 2 * block + half, pl.ds(start, 8, stride=stride), :]
                    for half in range(2)
                ],
                axis=1,
            )

        def fold_pair(pair, carry):
            def column(band, v):
                main = rows(band + 1, v, 16)
                if v < 10:
                    over = rows(band, 11 + v % 5 + 48 * (v // 5), 16)
                else:
                    over = rows(band, 96 + 11, 1)
                return main + jnp.where(tail_mask, over, 0.0)

            def residue_of(band, q):
                if q == 7:
                    return column(band, 8) + pltpu.roll(column(band, 0), 255, 1)
                if q < 2:
                    return column(band, q + 1) + pltpu.roll(column(band, q + 9), 1, 1)
                return column(band, q + 1)

            for q in range(8):
                value = jnp.concatenate(
                    [residue_of(2 * pair, q), residue_of(2 * pair + 1, q)], axis=0
                )
                high = value.astype(BF16)
                span = slice(q * 256, (q + 1) * 256)
                coeff[chan, pl.ds(pl.multiple_of(pair * 16, 16), 16), span] = high
                coeff[chan, pl.ds(pl.multiple_of(ROWS + pair * 16, 16), 16), span] = (
                    value - high.astype(F32)
                ).astype(BF16)
            return carry

        lax.fori_loop(0, 5, fold_pair, 0)

    def send_lines(chan):
        def line_group(step, carry):
            x, y = lat // 4 + step // 4, lat % 4 + step % 4
            far = (x + 2) % 4 * 4 + (y + 2) % 4
            near = x % 4 * 4 + y % 4
            weights = jnp.concatenate([lon_half[far], lon_half[near]], axis=1)
            product = jnp.dot(coeff[chan], weights, preferred_element_type=F32)
            total = (product[:ROWS] + product[ROWS:]).astype(BF16)
            for half, there in enumerate((far, near)):
                lines[chan, there] = total[:, half * 128 : (half + 1) * 128]
                copy = pltpu.make_async_remote_copy(
                    src_ref=lines.at[chan, there],
                    dst_ref=columns.at[chan, lat],
                    send_sem=line_send.at[chan],
                    recv_sem=line_recv.at[chan],
                    device_id=(there, lon),
                    device_id_type=MESH,
                )
                if half == 0:
                    copy.start()
                else:
                    pl.when(step > 0)(copy.start)

            return carry

        lax.fori_loop(0, 8, line_group, 0, unroll=2)

    def finish(chan):
        wait_for(columns.at[chan, pl.ds(0, LATS - 1)], line_recv.at[chan])
        columns[chan, lat] = lines[chan, lat]

        def assemble(source, carry):
            before = jnp.maximum(source - 1, 0)
            tail = columns[chan, before, 64:80, :].astype(F32)[0:8]
            for pair in range(4):
                value = columns[chan, source, pair * 16 : (pair + 1) * 16, :].astype(F32)
                start = pl.multiple_of(source * 64 + pair * 16, 16)
                if pair == 0:
                    column_sum[pl.ds(start, 8), :] = value[0:8] + jnp.where(source > 0, tail, 0.0)
                    column_sum[pl.ds(start + 8, 8), :] = value[8:16]
                else:
                    column_sum[pl.ds(start, 16), :] = value
            return carry

        lax.fori_loop(0, LATS, assemble, 0)
        column_sum[NLAT : NLAT + 8, :] = columns[chan, LATS - 1, 64:80, :].astype(F32)[0:8]
        whole = column_sum[1 : NLAT + 1, :].astype(BF16)
        for piece in range(4):
            span = slice(piece * 256, (piece + 1) * 256)
            high = jnp.concatenate([lat_high[part, span, :] for part in range(8)], axis=1)
            low_part = jnp.concatenate([lat_low[part, span, :] for part in range(8)], axis=1)
            out_ref[chan, span, :] = jnp.dot(high, whole, preferred_element_type=F32) + jnp.dot(
                low_part, whole, preferred_element_type=F32
            )

    wait_for(lat_raw, load_sem.at[1])
    lax.fori_loop(0, 8, prepare_lat, 0)
    lax.fori_loop(0, 8, send_group(1), 0)
    for group in range(4):
        add_group(0, group)
    fold(0)
    send_lines(0)
    for group in range(4):
        add_group(1, group)
    fold(1)
    send_lines(1)
    finish(0)
    finish(1)

    for chan in range(2):
        wait_for(got.at[chan, pl.ds(0, STEPS - 1)], send_sem.at[chan])
        wait_for(lines.at[chan, pl.ds(0, LATS - 1)], line_send.at[chan])


def on_device(cotangent, fractions, offsets, owner, sub_block, lon_inverse, lat_inverse):
    vmem = pl.BlockSpec(memory_space=pltpu.VMEM)
    hbm = pl.BlockSpec(memory_space=pltpu.HBM)
    operands = (
        cotangent, fractions, offsets, owner.reshape(1, BLOCKS), sub_block.reshape(1, BLOCKS),
        lon_inverse, lat_inverse,
    )
    return pl.pallas_call(
        kernel,
        out_shape=jax.ShapeDtypeStruct((2, NLAT, 128), F32),
        in_specs=[hbm] * 7,
        out_specs=vmem,
        scratch_shapes=[
            pltpu.VMEM((BLOCKS, CHANS, 128), BF16),
            pltpu.VMEM((BLOCKS, 2, 128), F32),
            pltpu.VMEM((BLOCKS, 2, 128), jnp.int32),
            pltpu.VMEM((1, BLOCKS), jnp.int32),
            pltpu.VMEM((1, BLOCKS), jnp.int32),
            pltpu.VMEM((8, 16, 128), F32),
            pltpu.VMEM((BLOCKS * CHANS, 128), F32),
            pltpu.VMEM((2, LONS, 256, 128), BF16),
            pltpu.VMEM((2, STEPS, PAIR, 128), BF16),
            pltpu.VMEM((2, 22, 176, 128), F32),
            pltpu.VMEM((2, 2 * ROWS, NLON), BF16),
            pltpu.VMEM((16, NLON, 128), F32),
            pltpu.VMEM((16, NLON, 128), BF16),
            pltpu.VMEM((NLAT, NLAT), F32),
            pltpu.VMEM((8, NLAT, 128), BF16),
            pltpu.VMEM((8, NLAT, 128), BF16),
            pltpu.VMEM((2, LATS, ROWS, 128), BF16),
            pltpu.VMEM((2, LATS, ROWS, 128), BF16),
            pltpu.VMEM((NLAT + 8, 128), F32),
            pltpu.SemaphoreType.REGULAR,
            pltpu.SemaphoreType.DMA((7,)),
            pltpu.SemaphoreType.DMA((2,)),
            pltpu.SemaphoreType.DMA((16,)),
            pltpu.SemaphoreType.DMA((2,)),
            pltpu.SemaphoreType.DMA((2,)),
        ],
        compiler_params=pltpu.CompilerParams(
            collective_id=0, has_side_effects=True, vmem_limit_bytes=50 * 2**20
        ),
    )(*(pltpu.with_memory_space_constraint(value, pltpu.HBM) for value in operands))


def solution(mesh):
    return jax.shard_map(
        on_device,
        mesh=mesh,
        in_specs=(
            P(("lat", "lon"), None, None),
            P(("lat", "lon"), None, None),
            P(("lat", "lon"), None, None),
            P(("lat", "lon"), None),
            P(("lat", "lon")),
            P(),
            P(),
        ),
        out_specs=P("lon", None, "lat"),
        check_vma=False,
    )
```

```python
import jax
import jax.numpy as jnp
from jax import lax
from jax.experimental import pallas as pl
from jax.experimental.pallas import tpu as pltpu
from jax.sharding import PartitionSpec as P

MESH = pl.DeviceIdType.MESH
F32 = jnp.float32
BF16 = jnp.bfloat16
LATS = 16
LONS = 8
BLOCKS = 128
CHANS = 16
NLAT = 1024
NLON = 2048
PAIR = 16
LABEL = 127
ROWS = 80
SELF = 8
STEPS = LATS * LONS


def spline(distance):
    size = jnp.abs(distance)
    far = jnp.maximum(2.0 - size, 0.0)
    near = jnp.maximum(1.0 - size, 0.0)
    return far * far * far - 4.0 * (near * near * near)


def wait_for(view, sem):
    pltpu.make_async_copy(view, view, sem).wait()


def kernel(cot_hbm, frac_hbm, off_hbm, owner_hbm, sub_hbm, lon_ref, lat_ref, out_ref,
           cot_ref, frac_ref, off_ref, owner_ref, sub_ref, lat_tab, windows, packed, got, summed, coeff, lon_raw, lon_half, lat_raw, lat_high,
           lat_low, lines, columns, column_sum,
           ready_sem, load_sem, send_sem, recv_sem, line_send, line_recv):
    lat, lon = lax.axis_index("lat"), lax.axis_index("lon")
    barrier = pltpu.get_barrier_semaphore()
    inputs = [
        pltpu.make_async_copy(source, target, load_sem.at[2 + place])
        for place, (source, target) in enumerate(
            (
                (cot_hbm, cot_ref),
                (frac_hbm, frac_ref),
                (off_hbm, off_ref),
                (owner_hbm, owner_ref),
                (sub_hbm, sub_ref),
            )
        )
    ]
    for copy in inputs:
        copy.start()

    lat_others = [
        (lat // 4 + dx) % 4 * 4 + (lat % 4 + dy) % 4
        for dx in range(4)
        for dy in range(4)
        if dx + dy > 0
    ]
    lon_there = [(lon // 2 + turn // 2) % 4 * 2 + (lon % 2 + turn % 2) % 2 for turn in range(8)]

    def greet(sem, lat_to, lon_to):
        pl.semaphore_signal(sem, inc=1, device_id=(lat_to, lon_to), device_id_type=MESH)

    for lat_to in lat_others:
        greet(barrier, lat_to, lon)
    for lon_to in lon_there[1:]:
        greet(barrier, lat, lon_to)

    for part in range(16):
        pltpu.make_async_copy(
            lon_ref.at[:, pl.ds(part * 128, 128)], lon_raw.at[part], load_sem.at[0]
        ).start()
    pltpu.make_async_copy(lat_ref, lat_raw, load_sem.at[1]).start()

    for copy in inputs:
        copy.wait()

    index = lax.broadcasted_iota(jnp.int32, (8, 128), 0)
    low = index.astype(F32)
    low_tail = index < 3
    head_end = index < 6

    def window_group(group, carry):
        places = off_ref[pl.ds(group * 8, 8)].astype(F32) + 1.0 + frac_ref[pl.ds(group * 8, 8)]
        stencils = []
        for item in range(8):
            centre_lat = jnp.broadcast_to(places[item, 0:1, :], (8, 128))
            centre_lon = jnp.broadcast_to(places[item, 1:2, :], (8, 128))
            lat_tail = spline(low + 8.0 - centre_lat) * (1.0 / 36.0)
            lat_tab[item, 0:8, :] = spline(low - centre_lat) * (1.0 / 36.0)
            lat_tab[item, 8:16, :] = lat_tail
            lon_head = spline(low - centre_lon)
            lon_tail = spline(low + 8.0 - centre_lon)
            lat_tab[item, 16:24, :] = lon_tail
            tail_a = jnp.where(low_tail, lon_tail, pltpu.roll(lon_head, 3, 0))
            tail_b = jnp.where(head_end, pltpu.roll(lon_head, 6, 0), pltpu.roll(lon_tail, 6, 0))
            tail_b = jnp.where(low_tail, lon_tail, tail_b)
            tail_c = jnp.where(
                low_tail, lon_tail, jnp.broadcast_to(lat_tab[item, 18:19, :], (8, 128))
            )
            lat_last = pltpu.roll(lat_tail, 3, 0)

            def lat_row(w):
                return jnp.broadcast_to(lat_tab[item, w : w + 1, :], (8, 128))

            high_rows = [lat_row(8), lat_row(9), lat_row(10)]
            pieces = []
            for w in range(8):
                row = lat_row(w)
                if w < 6:
                    tail_lat = jnp.where(low_tail, row, high_rows[w % 3])
                elif w == 6:
                    tail_lat = jnp.where(low_tail, row, lat_last)
                else:
                    tail_lat = row
                tail_lon = tail_a if w < 3 else (tail_b if w < 6 else tail_c)
                pieces.append(row * lon_head)
                pieces.append(tail_lat * tail_lon)
            stencils.append(jnp.concatenate(pieces, axis=0).astype(BF16))

        zero = jnp.zeros((CHANS, 128), BF16)
        for quad in range(2):
            four = [stencils[4 * quad + item] for item in range(4)]
            right = jnp.concatenate(
                [
                    jnp.concatenate([four[0], four[1]], axis=1),
                    jnp.concatenate([four[2], four[3]], axis=1),
                ],
                axis=0,
            )
            rows = []
            for item in range(4):
                grads = cot_ref[group * 8 + quad * 4 + item]
                rows.append(
                    jnp.concatenate([zero, grads] if item % 2 else [grads, zero], axis=1)
                )
            product = lax.dot_general(
                jnp.concatenate(rows, axis=0), right, (((1,), (1,)), ((), ())),
                preferred_element_type=F32,
            )
            first = pl.multiple_of(group * 128 + quad * 64, 64)
            windows[pl.ds(first, 32), :] = product[:32, :128]
            windows[pl.ds(first + 32, 32), :] = product[32:, 128:]
        return carry

    lax.fori_loop(0, 12, window_group, 0, unroll=4)

    pl.semaphore_wait(barrier, LATS - 1 + LONS - 1)

    for lon_to in lon_there[1:]:
        greet(ready_sem, lat, lon_to)
    lax.fori_loop(12, 16, window_group, 0, unroll=4)

    own_across = jnp.broadcast_to(owner_ref[...].astype(F32), (BLOCKS, BLOCKS))
    own_down = own_across.T
    down = lax.broadcasted_iota(jnp.int32, (BLOCKS, BLOCKS), 0)
    across = lax.broadcasted_iota(jnp.int32, (BLOCKS, BLOCKS), 1)
    earlier = jnp.where((own_down == own_across) & (down < across), 1.0, 0.0)
    place = 2.0 * own_across[0:1, :] + jnp.sum(earlier, axis=0, keepdims=True)
    slot = lax.broadcasted_iota(jnp.int32, (2 * BLOCKS, BLOCKS), 0).astype(F32)
    select = jnp.where(slot == place, 1.0, 0.0).astype(BF16)
    label = jnp.broadcast_to(sub_ref[...].astype(F32), (BLOCKS, BLOCKS)).T

    def pack(chan):
        for pair in range(0, LONS, 2):
            sides = []
            for lon_to in (pair, pair + 1):
                window = windows[pl.ds(2 * lon_to + chan, BLOCKS, stride=CHANS), :]
                sides.append(jnp.where(across == LABEL, label, window).astype(BF16))
            both = jnp.concatenate(sides, axis=1)
            slots = jnp.dot(select, both, preferred_element_type=F32).astype(BF16)
            packed[chan, pair] = slots[:, :128]
            packed[chan, pair + 1] = slots[:, 128:]
        start = pl.multiple_of(lat * PAIR, PAIR)
        got[chan, SELF] = packed[chan, lon, pl.ds(start, PAIR), :]

    def send_group(chan):
        def body(group, carry):
            for half in range(2):
                x = (lat // 4 + group // 4 + 2 - 2 * half) % 4
                y = (lat % 4 + group % 4 + 2 - 2 * half) % 4
                lat_to = x * 4 + y
                start = pl.multiple_of(lat_to * PAIR, PAIR)
                for turn in range(8):
                    step = group * 16 + half * 8 + turn
                    copy = pltpu.make_async_remote_copy(
                        src_ref=packed.at[chan, lon_there[turn], pl.ds(start, PAIR)],
                        dst_ref=got.at[chan, step],
                        send_sem=send_sem.at[chan],
                        recv_sem=recv_sem.at[chan * 8 + group],
                        device_id=(lat_to, lon_there[turn]),
                        device_id_type=MESH,
                    )
                    if half * 8 + turn == SELF:
                        pl.when(group > 0)(copy.start)
                    else:
                        copy.start()
            return carry

        return body

    pack(0)
    pl.semaphore_wait(ready_sem, LONS - 1)
    lax.fori_loop(0, 8, send_group(0), 0)
    pack(1)

    wait_for(lon_raw, load_sem.at[0])

    def prepare_lon(part, carry):
        for residue in range(8):
            rows = lon_raw[part, pl.ds(residue, 256, stride=8), :]
            lon_half[part, residue * 256 : (residue + 1) * 256, :] = rows.astype(BF16)
        return carry

    lax.fori_loop(0, 16, prepare_lon, 0)
    summed[...] = jnp.zeros_like(summed)

    def prepare_lat(part, carry):
        start = pl.multiple_of(part * 128, 128)
        for piece in range(8):
            turned = lat_raw[pl.ds(start, 128), piece * 128 : (piece + 1) * 128].T
            high = turned.astype(BF16)
            lat_high[part, piece * 128 : (piece + 1) * 128, :] = high
            lat_low[part, piece * 128 : (piece + 1) * 128, :] = (
                turned - high.astype(F32)
            ).astype(BF16)
        return carry

    lanes = lax.broadcasted_iota(jnp.int32, (256, 256), 1).astype(F32)
    tile = (lax.broadcasted_iota(jnp.int32, (256, 1), 0) // 2) % 4

    def add_group(chan, group):
        first = 32 * group
        if group == 0:
            wait_for(got.at[chan, pl.ds(0, 15)], recv_sem.at[chan * 8])
        else:
            wait_for(got.at[chan, pl.ds(first, 16)], recv_sem.at[chan * 8 + 2 * group])
        wait_for(got.at[chan, pl.ds(first + 16, 16)], recv_sem.at[chan * 8 + 2 * group + 1])
        chunk = got[chan, first : first + 32].astype(F32)
        for half in range(2):
            part = chunk[:, 8 * half : 8 * half + 8, :].reshape(256, 128)
            name = part[:, LABEL : LABEL + 1].astype(jnp.int32)
            goal = ((name // 32) * 128 + tile * 32 + name % 32).astype(F32)
            goal = jnp.broadcast_to(goal, (256, 256)) - lanes
            turned = part.T.astype(BF16)
            for pair in range(4):
                match = jnp.where(goal == float(pair * 256), 1.0, 0.0).astype(BF16)
                add = jnp.dot(turned, match, preferred_element_type=F32)
                summed[chan, 4 * pair + 2 + half, 0:128, :] += add[:, :128]
                summed[chan, 4 * pair + 4 + half, 0:128, :] += add[:, 128:]

    tail_mask = lax.broadcasted_iota(jnp.int32, (8, 256), 0) < 3

    def fold(chan):
        def rows(block, start, stride):
            return jnp.concatenate(
                [
                    summed[chan, 2 * block + half, pl.ds(start, 8, stride=stride), :]
                    for half in range(2)
                ],
                axis=1,
            )

        def fold_pair(pair, carry):
            def column(band, v):
                main = rows(band + 1, v, 16)
                if v < 10:
                    over = rows(band, 11 + v % 5 + 48 * (v // 5), 16)
                else:
                    over = rows(band, 96 + 11, 1)
                return main + jnp.where(tail_mask, over, 0.0)

            def residue_of(band, q):
                if q == 7:
                    return column(band, 8) + pltpu.roll(column(band, 0), 255, 1)
                if q < 2:
                    return column(band, q + 1) + pltpu.roll(column(band, q + 9), 1, 1)
                return column(band, q + 1)

            for q in range(8):
                value = jnp.concatenate(
                    [residue_of(2 * pair, q), residue_of(2 * pair + 1, q)], axis=0
                )
                high = value.astype(BF16)
                span = slice(q * 256, (q + 1) * 256)
                coeff[chan, pl.ds(pl.multiple_of(pair * 16, 16), 16), span] = high
                coeff[chan, pl.ds(pl.multiple_of(ROWS + pair * 16, 16), 16), span] = (
                    value - high.astype(F32)
                ).astype(BF16)
            return carry

        lax.fori_loop(0, 5, fold_pair, 0, unroll=5)

    def send_lines(chan):
        def line_group(step, carry):
            x, y = lat // 4 + step // 4, lat % 4 + step % 4
            far = (x + 2) % 4 * 4 + (y + 2) % 4
            near = x % 4 * 4 + y % 4
            weights = jnp.concatenate([lon_half[far], lon_half[near]], axis=1)
            product = jnp.dot(coeff[chan], weights, preferred_element_type=F32)
            total = (product[:ROWS] + product[ROWS:]).astype(BF16)
            for half, there in enumerate((far, near)):
                lines[chan, there] = total[:, half * 128 : (half + 1) * 128]
                copy = pltpu.make_async_remote_copy(
                    src_ref=lines.at[chan, there],
                    dst_ref=columns.at[chan, lat],
                    send_sem=line_send.at[chan],
                    recv_sem=line_recv.at[chan],
                    device_id=(there, lon),
                    device_id_type=MESH,
                )
                if half == 0:
                    copy.start()
                else:
                    pl.when(step > 0)(copy.start)

            return carry

        lax.fori_loop(0, 8, line_group, 0, unroll=2)

    def finish(chan):
        wait_for(columns.at[chan, pl.ds(0, LATS - 1)], line_recv.at[chan])
        columns[chan, lat] = lines[chan, lat]

        def assemble(source, carry):
            before = jnp.maximum(source - 1, 0)
            tail = columns[chan, before, 64:80, :].astype(F32)[0:8]
            for pair in range(4):
                value = columns[chan, source, pair * 16 : (pair + 1) * 16, :].astype(F32)
                start = pl.multiple_of(source * 64 + pair * 16, 16)
                if pair == 0:
                    column_sum[pl.ds(start, 8), :] = value[0:8] + jnp.where(source > 0, tail, 0.0)
                    column_sum[pl.ds(start + 8, 8), :] = value[8:16]
                else:
                    column_sum[pl.ds(start, 16), :] = value
            return carry

        lax.fori_loop(0, LATS, assemble, 0, unroll=4)
        column_sum[NLAT : NLAT + 8, :] = columns[chan, LATS - 1, 64:80, :].astype(F32)[0:8]
        whole = column_sum[1 : NLAT + 1, :].astype(BF16)
        for piece in range(4):
            span = slice(piece * 256, (piece + 1) * 256)
            high = jnp.concatenate([lat_high[part, span, :] for part in range(8)], axis=1)
            low_part = jnp.concatenate([lat_low[part, span, :] for part in range(8)], axis=1)
            out_ref[chan, span, :] = jnp.dot(high, whole, preferred_element_type=F32) + jnp.dot(
                low_part, whole, preferred_element_type=F32
            )

    wait_for(lat_raw, load_sem.at[1])
    lax.fori_loop(0, 8, prepare_lat, 0)
    lax.fori_loop(0, 8, send_group(1), 0)
    for group in range(4):
        add_group(0, group)
    fold(0)
    send_lines(0)
    for group in range(4):
        add_group(1, group)
    fold(1)
    send_lines(1)
    finish(0)
    finish(1)

    for chan in range(2):
        wait_for(got.at[chan, pl.ds(0, STEPS - 1)], send_sem.at[chan])
        wait_for(lines.at[chan, pl.ds(0, LATS - 1)], line_send.at[chan])


def on_device(cotangent, fractions, offsets, owner, sub_block, lon_inverse, lat_inverse):
    vmem = pl.BlockSpec(memory_space=pltpu.VMEM)
    hbm = pl.BlockSpec(memory_space=pltpu.HBM)
    operands = (
        cotangent, fractions, offsets, owner.reshape(1, BLOCKS), sub_block.reshape(1, BLOCKS),
        lon_inverse, lat_inverse,
    )
    return pl.pallas_call(
        kernel,
        out_shape=jax.ShapeDtypeStruct((2, NLAT, 128), F32),
        in_specs=[hbm] * 7,
        out_specs=vmem,
        scratch_shapes=[
            pltpu.VMEM((BLOCKS, CHANS, 128), BF16),
            pltpu.VMEM((BLOCKS, 2, 128), F32),
            pltpu.VMEM((BLOCKS, 2, 128), jnp.int32),
            pltpu.VMEM((1, BLOCKS), jnp.int32),
            pltpu.VMEM((1, BLOCKS), jnp.int32),
            pltpu.VMEM((8, 24, 128), F32),
            pltpu.VMEM((BLOCKS * CHANS, 128), F32),
            pltpu.VMEM((2, LONS, 256, 128), BF16),
            pltpu.VMEM((2, STEPS, PAIR, 128), BF16),
            pltpu.VMEM((2, 22, 176, 128), F32),
            pltpu.VMEM((2, 2 * ROWS, NLON), BF16),
            pltpu.VMEM((16, NLON, 128), F32),
            pltpu.VMEM((16, NLON, 128), BF16),
            pltpu.VMEM((NLAT, NLAT), F32),
            pltpu.VMEM((8, NLAT, 128), BF16),
            pltpu.VMEM((8, NLAT, 128), BF16),
            pltpu.VMEM((2, LATS, ROWS, 128), BF16),
            pltpu.VMEM((2, LATS, ROWS, 128), BF16),
            pltpu.VMEM((NLAT + 8, 128), F32),
            pltpu.SemaphoreType.REGULAR,
            pltpu.SemaphoreType.DMA((7,)),
            pltpu.SemaphoreType.DMA((2,)),
            pltpu.SemaphoreType.DMA((16,)),
            pltpu.SemaphoreType.DMA((2,)),
            pltpu.SemaphoreType.DMA((2,)),
        ],
        compiler_params=pltpu.CompilerParams(
            collective_id=0, has_side_effects=True, vmem_limit_bytes=50 * 2**20
        ),
    )(*(pltpu.with_memory_space_constraint(value, pltpu.HBM) for value in operands))


def solution(mesh):
    return jax.shard_map(
        on_device,
        mesh=mesh,
        in_specs=(
            P(("lat", "lon"), None, None),
            P(("lat", "lon"), None, None),
            P(("lat", "lon"), None, None),
            P(("lat", "lon"), None),
            P(("lat", "lon")),
            P(),
            P(),
        ),
        out_specs=P("lon", None, "lat"),
        check_vma=False,
    )
```

```python
import jax
import jax.numpy as jnp
from jax import lax
from jax.experimental import pallas as pl
from jax.experimental.pallas import tpu as pltpu
from jax.sharding import PartitionSpec as P

MESH = pl.DeviceIdType.MESH
F32 = jnp.float32
BF16 = jnp.bfloat16
LATS = 16
LONS = 8
BLOCKS = 128
CHANS = 16
NLAT = 1024
NLON = 2048
PAIR = 16
LABEL = 127
ROWS = 80
SELF = 8
STEPS = LATS * LONS


def spline(distance):
    size = jnp.abs(distance)
    far = jnp.maximum(2.0 - size, 0.0)
    near = jnp.maximum(1.0 - size, 0.0)
    return far * far * far - 4.0 * (near * near * near)


def wait_for(view, sem):
    pltpu.make_async_copy(view, view, sem).wait()


def kernel(cot_hbm, frac_hbm, off_hbm, owner_hbm, sub_hbm, lon_ref, lat_ref, out_ref,
           cot_ref, frac_ref, off_ref, owner_ref, sub_ref, lat_tab, windows, packed, got, summed, coeff, lon_raw, lon_half, lat_raw, lat_high,
           lat_low, lines, columns, column_sum,
           ready_sem, load_sem, send_sem, recv_sem, line_send, line_recv):
    lat, lon = lax.axis_index("lat"), lax.axis_index("lon")
    barrier = pltpu.get_barrier_semaphore()
    inputs = [
        pltpu.make_async_copy(source, target, load_sem.at[2 + place])
        for place, (source, target) in enumerate(
            (
                (cot_hbm, cot_ref),
                (frac_hbm, frac_ref),
                (off_hbm, off_ref),
                (owner_hbm, owner_ref),
                (sub_hbm, sub_ref),
            )
        )
    ]
    for copy in inputs:
        copy.start()

    lat_others = [
        (lat // 4 + dx) % 4 * 4 + (lat % 4 + dy) % 4
        for dx in range(4)
        for dy in range(4)
        if dx + dy > 0
    ]
    lon_there = [(lon // 2 + turn // 2) % 4 * 2 + (lon % 2 + turn % 2) % 2 for turn in range(8)]

    def greet(sem, lat_to, lon_to):
        pl.semaphore_signal(sem, inc=1, device_id=(lat_to, lon_to), device_id_type=MESH)

    for lat_to in lat_others:
        greet(barrier, lat_to, lon)
    for lon_to in lon_there[1:]:
        greet(barrier, lat, lon_to)

    for part in range(16):
        pltpu.make_async_copy(
            lon_ref.at[:, pl.ds(part * 128, 128)], lon_raw.at[part], load_sem.at[0]
        ).start()
    pltpu.make_async_copy(lat_ref, lat_raw, load_sem.at[1]).start()

    for copy in inputs:
        copy.wait()

    index = lax.broadcasted_iota(jnp.int32, (8, 128), 0)
    low = index.astype(F32)
    low_tail = index < 3
    head_end = index < 6

    def window_group(group, carry):
        places = off_ref[pl.ds(group * 8, 8)].astype(F32) + 1.0 + frac_ref[pl.ds(group * 8, 8)]
        stencils = []
        for item in range(8):
            centre_lat = jnp.broadcast_to(places[item, 0:1, :], (8, 128))
            centre_lon = jnp.broadcast_to(places[item, 1:2, :], (8, 128))
            lat_tail = spline(low + 8.0 - centre_lat) * (1.0 / 36.0)
            lat_tab[item, 0:8, :] = spline(low - centre_lat) * (1.0 / 36.0)
            lat_tab[item, 8:16, :] = lat_tail
            lon_head = spline(low - centre_lon)
            lon_tail = spline(low + 8.0 - centre_lon)
            lat_tab[item, 16:24, :] = lon_tail
            tail_a = jnp.where(low_tail, lon_tail, pltpu.roll(lon_head, 3, 0))
            tail_b = jnp.where(head_end, pltpu.roll(lon_head, 6, 0), pltpu.roll(lon_tail, 6, 0))
            tail_b = jnp.where(low_tail, lon_tail, tail_b)
            tail_c = jnp.where(
                low_tail, lon_tail, jnp.broadcast_to(lat_tab[item, 18:19, :], (8, 128))
            )
            lat_last = pltpu.roll(lat_tail, 3, 0)

            def lat_row(w):
                return jnp.broadcast_to(lat_tab[item, w : w + 1, :], (8, 128))

            high_rows = [lat_row(8), lat_row(9), lat_row(10)]
            pieces = []
            for w in range(8):
                row = lat_row(w)
                if w < 6:
                    tail_lat = jnp.where(low_tail, row, high_rows[w % 3])
                elif w == 6:
                    tail_lat = jnp.where(low_tail, row, lat_last)
                else:
                    tail_lat = row
                tail_lon = tail_a if w < 3 else (tail_b if w < 6 else tail_c)
                pieces.append(row * lon_head)
                pieces.append(tail_lat * tail_lon)
            stencils.append(jnp.concatenate(pieces, axis=0).astype(BF16))

        zero = jnp.zeros((CHANS, 128), BF16)
        for quad in range(2):
            four = [stencils[4 * quad + item] for item in range(4)]
            right = jnp.concatenate(
                [
                    jnp.concatenate([four[0], four[1]], axis=1),
                    jnp.concatenate([four[2], four[3]], axis=1),
                ],
                axis=0,
            )
            rows = []
            for item in range(4):
                grads = cot_ref[group * 8 + quad * 4 + item]
                rows.append(
                    jnp.concatenate([zero, grads] if item % 2 else [grads, zero], axis=1)
                )
            product = lax.dot_general(
                jnp.concatenate(rows, axis=0), right, (((1,), (1,)), ((), ())),
                preferred_element_type=F32,
            )
            first = pl.multiple_of(group * 128 + quad * 64, 64)
            windows[pl.ds(first, 32), :] = product[:32, :128]
            windows[pl.ds(first + 32, 32), :] = product[32:, 128:]
        return carry

    lax.fori_loop(0, 8, window_group, 0, unroll=4)

    pl.semaphore_wait(barrier, LATS - 1 + LONS - 1)

    for lon_to in lon_there[1:]:
        greet(ready_sem, lat, lon_to)
    lax.fori_loop(8, 16, window_group, 0, unroll=4)

    own_across = jnp.broadcast_to(owner_ref[...].astype(F32), (BLOCKS, BLOCKS))
    own_down = own_across.T
    down = lax.broadcasted_iota(jnp.int32, (BLOCKS, BLOCKS), 0)
    across = lax.broadcasted_iota(jnp.int32, (BLOCKS, BLOCKS), 1)
    earlier = jnp.where((own_down == own_across) & (down < across), 1.0, 0.0)
    place = 2.0 * own_across[0:1, :] + jnp.sum(earlier, axis=0, keepdims=True)
    slot = lax.broadcasted_iota(jnp.int32, (2 * BLOCKS, BLOCKS), 0).astype(F32)
    select = jnp.where(slot == place, 1.0, 0.0).astype(BF16)
    label = jnp.broadcast_to(sub_ref[...].astype(F32), (BLOCKS, BLOCKS)).T

    def pack(chan):
        for pair in range(0, LONS, 2):
            sides = []
            for lon_to in (pair, pair + 1):
                window = windows[pl.ds(2 * lon_to + chan, BLOCKS, stride=CHANS), :]
                sides.append(jnp.where(across == LABEL, label, window).astype(BF16))
            both = jnp.concatenate(sides, axis=1)
            slots = jnp.dot(select, both, preferred_element_type=F32).astype(BF16)
            packed[chan, pair] = slots[:, :128]
            packed[chan, pair + 1] = slots[:, 128:]
        start = pl.multiple_of(lat * PAIR, PAIR)
        got[chan, SELF] = packed[chan, lon, pl.ds(start, PAIR), :]

    def send_group(chan):
        def body(group, carry):
            for half in range(2):
                x = (lat // 4 + group // 4 + 2 - 2 * half) % 4
                y = (lat % 4 + group % 4 + 2 - 2 * half) % 4
                lat_to = x * 4 + y
                start = pl.multiple_of(lat_to * PAIR, PAIR)
                for turn in range(8):
                    step = group * 16 + half * 8 + turn
                    copy = pltpu.make_async_remote_copy(
                        src_ref=packed.at[chan, lon_there[turn], pl.ds(start, PAIR)],
                        dst_ref=got.at[chan, step],
                        send_sem=send_sem.at[chan],
                        recv_sem=recv_sem.at[chan * 8 + group],
                        device_id=(lat_to, lon_there[turn]),
                        device_id_type=MESH,
                    )
                    if half * 8 + turn == SELF:
                        pl.when(group > 0)(copy.start)
                    else:
                        copy.start()
            return carry

        return body

    pack(0)
    pl.semaphore_wait(ready_sem, LONS - 1)
    lax.fori_loop(0, 8, send_group(0), 0)
    pack(1)

    wait_for(lon_raw, load_sem.at[0])

    def prepare_lon(part, carry):
        for residue in range(8):
            rows = lon_raw[part, pl.ds(residue, 256, stride=8), :]
            lon_half[part, residue * 256 : (residue + 1) * 256, :] = rows.astype(BF16)
        return carry

    lax.fori_loop(0, 16, prepare_lon, 0)
    summed[...] = jnp.zeros_like(summed)

    def prepare_lat(part, carry):
        start = pl.multiple_of(part * 128, 128)
        for piece in range(8):
            turned = lat_raw[pl.ds(start, 128), piece * 128 : (piece + 1) * 128].T
            high = turned.astype(BF16)
            lat_high[part, piece * 128 : (piece + 1) * 128, :] = high
            lat_low[part, piece * 128 : (piece + 1) * 128, :] = (
                turned - high.astype(F32)
            ).astype(BF16)
        return carry

    lanes = lax.broadcasted_iota(jnp.int32, (256, 256), 1).astype(F32)
    tile = (lax.broadcasted_iota(jnp.int32, (256, 1), 0) // 2) % 4

    def add_group(chan, group):
        first = 32 * group
        if group == 0:
            wait_for(got.at[chan, pl.ds(0, 15)], recv_sem.at[chan * 8])
        else:
            wait_for(got.at[chan, pl.ds(first, 16)], recv_sem.at[chan * 8 + 2 * group])
        wait_for(got.at[chan, pl.ds(first + 16, 16)], recv_sem.at[chan * 8 + 2 * group + 1])
        chunk = got[chan, first : first + 32].astype(F32)
        for half in range(2):
            part = chunk[:, 8 * half : 8 * half + 8, :].reshape(256, 128)
            name = part[:, LABEL : LABEL + 1].astype(jnp.int32)
            goal = ((name // 32) * 128 + tile * 32 + name % 32).astype(F32)
            goal = jnp.broadcast_to(goal, (256, 256)) - lanes
            turned = part.T.astype(BF16)
            for pair in range(4):
                match = jnp.where(goal == float(pair * 256), 1.0, 0.0).astype(BF16)
                add = jnp.dot(turned, match, preferred_element_type=F32)
                summed[chan, 4 * pair + 2 + half, 0:128, :] += add[:, :128]
                summed[chan, 4 * pair + 4 + half, 0:128, :] += add[:, 128:]

    tail_mask = lax.broadcasted_iota(jnp.int32, (8, 256), 0) < 3

    def fold(chan):
        def rows(block, start, stride):
            return jnp.concatenate(
                [
                    summed[chan, 2 * block + half, pl.ds(start, 8, stride=stride), :]
                    for half in range(2)
                ],
                axis=1,
            )

        def fold_pair(pair, carry):
            def column(band, v):
                main = rows(band + 1, v, 16)
                if v < 10:
                    over = rows(band, 11 + v % 5 + 48 * (v // 5), 16)
                else:
                    over = rows(band, 96 + 11, 1)
                return main + jnp.where(tail_mask, over, 0.0)

            def residue_of(band, q):
                if q == 7:
                    return column(band, 8) + pltpu.roll(column(band, 0), 255, 1)
                if q < 2:
                    return column(band, q + 1) + pltpu.roll(column(band, q + 9), 1, 1)
                return column(band, q + 1)

            for q in range(8):
                value = jnp.concatenate(
                    [residue_of(2 * pair, q), residue_of(2 * pair + 1, q)], axis=0
                )
                high = value.astype(BF16)
                span = slice(q * 256, (q + 1) * 256)
                coeff[chan, pl.ds(pl.multiple_of(pair * 16, 16), 16), span] = high
                coeff[chan, pl.ds(pl.multiple_of(ROWS + pair * 16, 16), 16), span] = (
                    value - high.astype(F32)
                ).astype(BF16)
            return carry

        lax.fori_loop(0, 5, fold_pair, 0, unroll=5)

    def send_lines(chan):
        def line_group(step, carry):
            x, y = lat // 4 + step // 4, lat % 4 + step % 4
            far = (x + 2) % 4 * 4 + (y + 2) % 4
            near = x % 4 * 4 + y % 4
            weights = jnp.concatenate([lon_half[far], lon_half[near]], axis=1)
            product = jnp.dot(coeff[chan], weights, preferred_element_type=F32)
            total = (product[:ROWS] + product[ROWS:]).astype(BF16)
            for half, there in enumerate((far, near)):
                lines[chan, there] = total[:, half * 128 : (half + 1) * 128]
                copy = pltpu.make_async_remote_copy(
                    src_ref=lines.at[chan, there],
                    dst_ref=columns.at[chan, lat],
                    send_sem=line_send.at[chan],
                    recv_sem=line_recv.at[chan],
                    device_id=(there, lon),
                    device_id_type=MESH,
                )
                if half == 0:
                    copy.start()
                else:
                    pl.when(step > 0)(copy.start)

            return carry

        lax.fori_loop(0, 8, line_group, 0, unroll=8)

    def finish(chan):
        wait_for(columns.at[chan, pl.ds(0, LATS - 1)], line_recv.at[chan])
        columns[chan, lat] = lines[chan, lat]

        def assemble(source, carry):
            before = jnp.maximum(source - 1, 0)
            tail = columns[chan, before, 64:80, :].astype(F32)[0:8]
            for pair in range(4):
                value = columns[chan, source, pair * 16 : (pair + 1) * 16, :].astype(F32)
                start = pl.multiple_of(source * 64 + pair * 16, 16)
                if pair == 0:
                    column_sum[pl.ds(start, 8), :] = value[0:8] + jnp.where(source > 0, tail, 0.0)
                    column_sum[pl.ds(start + 8, 8), :] = value[8:16]
                else:
                    column_sum[pl.ds(start, 16), :] = value
            return carry

        lax.fori_loop(0, LATS, assemble, 0, unroll=4)
        column_sum[NLAT : NLAT + 8, :] = columns[chan, LATS - 1, 64:80, :].astype(F32)[0:8]
        whole = column_sum[1 : NLAT + 1, :].astype(BF16)
        for piece in range(4):
            span = slice(piece * 256, (piece + 1) * 256)
            high = jnp.concatenate([lat_high[part, span, :] for part in range(8)], axis=1)
            low_part = jnp.concatenate([lat_low[part, span, :] for part in range(8)], axis=1)
            out_ref[chan, span, :] = jnp.dot(high, whole, preferred_element_type=F32) + jnp.dot(
                low_part, whole, preferred_element_type=F32
            )

    wait_for(lat_raw, load_sem.at[1])
    lax.fori_loop(0, 8, prepare_lat, 0)
    lax.fori_loop(0, 8, send_group(1), 0)
    for group in range(4):
        add_group(0, group)
    fold(0)
    send_lines(0)
    for group in range(4):
        add_group(1, group)
    fold(1)
    send_lines(1)
    finish(0)
    finish(1)

    for chan in range(2):
        wait_for(got.at[chan, pl.ds(0, STEPS - 1)], send_sem.at[chan])
        wait_for(lines.at[chan, pl.ds(0, LATS - 1)], line_send.at[chan])


def on_device(cotangent, fractions, offsets, owner, sub_block, lon_inverse, lat_inverse):
    vmem = pl.BlockSpec(memory_space=pltpu.VMEM)
    hbm = pl.BlockSpec(memory_space=pltpu.HBM)
    operands = (
        cotangent, fractions, offsets, owner.reshape(1, BLOCKS), sub_block.reshape(1, BLOCKS),
        lon_inverse, lat_inverse,
    )
    return pl.pallas_call(
        kernel,
        out_shape=jax.ShapeDtypeStruct((2, NLAT, 128), F32),
        in_specs=[hbm] * 7,
        out_specs=vmem,
        scratch_shapes=[
            pltpu.VMEM((BLOCKS, CHANS, 128), BF16),
            pltpu.VMEM((BLOCKS, 2, 128), F32),
            pltpu.VMEM((BLOCKS, 2, 128), jnp.int32),
            pltpu.VMEM((1, BLOCKS), jnp.int32),
            pltpu.VMEM((1, BLOCKS), jnp.int32),
            pltpu.VMEM((8, 24, 128), F32),
            pltpu.VMEM((BLOCKS * CHANS, 128), F32),
            pltpu.VMEM((2, LONS, 256, 128), BF16),
            pltpu.VMEM((2, STEPS, PAIR, 128), BF16),
            pltpu.VMEM((2, 22, 176, 128), F32),
            pltpu.VMEM((2, 2 * ROWS, NLON), BF16),
            pltpu.VMEM((16, NLON, 128), F32),
            pltpu.VMEM((16, NLON, 128), BF16),
            pltpu.VMEM((NLAT, NLAT), F32),
            pltpu.VMEM((8, NLAT, 128), BF16),
            pltpu.VMEM((8, NLAT, 128), BF16),
            pltpu.VMEM((2, LATS, ROWS, 128), BF16),
            pltpu.VMEM((2, LATS, ROWS, 128), BF16),
            pltpu.VMEM((NLAT + 8, 128), F32),
            pltpu.SemaphoreType.REGULAR,
            pltpu.SemaphoreType.DMA((7,)),
            pltpu.SemaphoreType.DMA((2,)),
            pltpu.SemaphoreType.DMA((16,)),
            pltpu.SemaphoreType.DMA((2,)),
            pltpu.SemaphoreType.DMA((2,)),
        ],
        compiler_params=pltpu.CompilerParams(
            collective_id=0, has_side_effects=True, vmem_limit_bytes=50 * 2**20
        ),
    )(*(pltpu.with_memory_space_constraint(value, pltpu.HBM) for value in operands))


def solution(mesh):
    return jax.shard_map(
        on_device,
        mesh=mesh,
        in_specs=(
            P(("lat", "lon"), None, None),
            P(("lat", "lon"), None, None),
            P(("lat", "lon"), None, None),
            P(("lat", "lon"), None),
            P(("lat", "lon")),
            P(),
            P(),
        ),
        out_specs=P("lon", None, "lat"),
        check_vma=False,
    )
```
